128 devices in a mesh: rep: 8 (over y, x_hi), fsdp: 16 (over z, x_lo, core).
Axes of the slice: x: 4 (x_hi: 2, x_lo: 2; x = x_hi * 2 + x_lo), y: 4, z: 4, core: 2. Of those that a mesh axis runs over, the one named last changes fastest.
Arguments:
- step_bit: int32 [], replicated, may hold values from 0 to 999
- tokens: bfloat16 [8, 16384, 5120], P('rep', 'fsdp'), may hold values from -6 to 6
- target: bfloat16 [8, 16384, 1024], P('rep', 'fsdp'), may hold values from -6 to 6
- norm_gain: float32 [5120], replicated, may hold values from 0.5 to 2
- weights: bfloat16 [8, 5120, 1024], P('rep', 'fsdp')
- previous: bfloat16 [8, 5120, 1024], P('rep', 'fsdp')
- anchor: float32 [8, 5120, 1024], P('rep', 'fsdp')
- momentum: float32 [8, 5120, 1024], P('rep', 'fsdp'), may hold values from -6 to 6
Outputs:
- new_momentum: float32 [8, 5120, 1024], P('rep', 'fsdp')
- new_anchor: float32 [8, 5120, 1024], P('rep', 'fsdp')
The draws below stay inside these ranges and needn't reach their ends.
All inputs are finite; a program needn't handle non-finite values.
Results may differ from the reference program's by a relative error of at most 0.0022.
Values may be sent and summed in bfloat16 or wider, within the bound.
A program may use at most 192 MiB of HBM per device.

```python
import math
import jax
import jax.numpy as jnp
from jax import lax

D = 5120
KV_WIDTH = 1024
TOKENS = 16384
REPS = 8


def shared_base(key):
    single = jax.random.normal(key, (D, KV_WIDTH), jnp.float32)
    return jnp.broadcast_to(single[None], (REPS, D, KV_WIDTH))


def noise_field(key):
    return jax.random.normal(key, (REPS, D, KV_WIDTH), jnp.float32)


def draw_weights(key, part):
    base = shared_base(key)
    key = jax.random.fold_in(key, 11)
    return (base + 0.05 * noise_field(key)).astype(jnp.bfloat16)


def draw_previous(key, part):
    base = shared_base(key)
    key = jax.random.fold_in(key, 23)
    return (base + 0.05 * noise_field(key)).astype(jnp.bfloat16)


def draw_anchor(key, part):
    base = shared_base(key)
    key = jax.random.fold_in(key, 37)
    return base + 0.05 * noise_field(key)


def steps_of(rng, dims, pieces, smallest, largest):
    def one(axis_at, parts):
        steps = jax.random.uniform(jax.random.fold_in(jax.random.fold_in(rng, 6), axis_at), (parts,), jnp.float32, smallest / len(pieces), largest / len(pieces))
        return jnp.repeat(jnp.exp(steps), dims[axis_at] // parts).reshape((-1,) + (1,) * (len(dims) - axis_at - 1))

    factor_of = one(*pieces[0])
    for cut in pieces[1:]:
        factor_of = factor_of * one(*cut)
    return factor_of


def normal_values(rng, shape, width, most, shards=(), held_as=jnp.bfloat16):
    array = width * jax.random.normal(rng, shape, jnp.float32)
    if shards:
        array = array * steps_of(rng, shape, shards, -0.22, 0.18)
    return jnp.clip(array, -most, most).astype(held_as)


def setup_inputs(seed: int = 0) -> dict:
    key_of = jax.random.split(jax.random.key(seed), 9)
    step_bit = jax.random.randint(key_of[0], (), 0, 1000).astype(jnp.int32)
    tokens = normal_values(key_of[1], (REPS, TOKENS, D), 1.0, 6.0, ((0, 8), (1, 16)))
    target = normal_values(key_of[2], (REPS, TOKENS, KV_WIDTH), 1.0, 6.0, ((0, 8), (1, 16)))
    norm_gain = jnp.clip(jnp.exp(jax.random.uniform(key_of[3], (D,), jnp.float32, math.log(0.5), math.log(2.0))), 0.5, 2.0)
    weights = draw_weights(jax.random.fold_in(key_of[8], 71), 0)
    previous = draw_previous(jax.random.fold_in(key_of[8], 71), 0)
    anchor = draw_anchor(jax.random.fold_in(key_of[8], 71), 0)
    momentum = normal_values(key_of[7], (REPS, D, KV_WIDTH), 1.0, 6.0, ((0, 8), (1, 16)), jnp.float32)
    return dict(step_bit=step_bit, tokens=tokens, target=target, norm_gain=norm_gain, weights=weights, previous=previous, anchor=anchor, momentum=momentum)


EPS = 1e-06
INNER_RATE = 0.05
OUTER_RATE = 1.0
SLOW_BETA = 0.6

def reference(step_bit, tokens, target, norm_gain, weights, previous, anchor, momentum):
    moment_list = []
    anchor_list = []
    bit_count = REPS.bit_length() - 1
    chosen_bit = jnp.remainder(step_bit.astype(jnp.int32), jnp.int32(bit_count)).astype(jnp.int32)
    shift_mask = jnp.left_shift(jnp.int32(1), chosen_bit)
    for replica in range(REPS):
        token_rows = tokens[replica].astype(jnp.float32)
        scale_rms = lax.rsqrt(lax.optimization_barrier(jnp.mean(token_rows * token_rows, axis=-1, keepdims=True)) + EPS)
        normed = (token_rows * scale_rms * norm_gain).astype(jnp.bfloat16)
        values = jnp.dot(normed, weights[replica], preferred_element_type=jnp.float32) * D ** (-0.5)
        error = (values - target[replica].astype(jnp.float32)).astype(jnp.bfloat16)
        gradient = jnp.dot(normed.T, error, preferred_element_type=jnp.float32) * D ** (-0.5)
        fast_weights = weights[replica].astype(jnp.float32) - INNER_RATE * gradient
        partner = jnp.bitwise_xor(jnp.int32(replica), shift_mask).astype(jnp.int32)
        partner_weights = lax.dynamic_index_in_dim(previous, partner, 0, keepdims=False)
        mixed = 0.5 * fast_weights + 0.5 * partner_weights.astype(jnp.float32)
        moment_new = SLOW_BETA * momentum[replica] + (anchor[replica] - mixed) / INNER_RATE
        anchor_new = anchor[replica] - OUTER_RATE * INNER_RATE * moment_new
        moment_list.append(moment_new)
        anchor_list.append(anchor_new)
    return (jnp.stack(moment_list), jnp.stack(anchor_list))
```

```python
import functools

import jax
import jax.numpy as jnp
from jax import lax
from jax.experimental import pallas as pl
from jax.experimental.pallas import tpu as pltpu
from jax.sharding import PartitionSpec as P

EPS = 1e-06
INNER_RATE = 0.05
OUTER_RATE = 1.0
SLOW_BETA = 0.6

MESH = pl.DeviceIdType.MESH
BF16 = jnp.bfloat16
F32 = jnp.float32

ROWS = 320
BLOCK = 2 * ROWS
CHUNK = 256
CHUNKS = 2
TILE = 128
STEP = 512
N_AG = 15
N_RS = 26


def kernel(
    mask,
    p_rows,
    tokens,
    target,
    gain,
    weights,
    previous,
    anchor,
    momentum,
    new_momentum,
    new_anchor,
    normed,
    full,
    grad,
    grad_half,
    tgt,
    err,
    from_mate,
    far,
    near,
    mate_p,
    total,
    swapped,
    own_w,
    partner,
    anchor_v,
    momentum_v,
    gain_v,
    ag_send,
    ag_recv,
    rs_send,
    rs_recv,
    n_send,
    n_recv,
    m_send,
    m_recv,
    local,
):
    rep = lax.axis_index("rep")
    at = lax.axis_index("fsdp")
    core = lax.rem(at, 2)
    other = 1 - core
    x = lax.rem(at // 2, 2)
    z = at // 4
    z_up, z_down, z_far = lax.rem(z + 1, 4), lax.rem(z + 3, 4), lax.rem(z + 2, 4)
    up = (rep, z_up * 4 + x * 2 + core)
    down = (rep, z_down * 4 + x * 2 + core)
    mate = (rep, z * 4 + (1 - x) * 2 + core)
    sibling = (rep, z * 4 + x * 2 + other)
    friend = (rep + mask - 2 * mask * lax.rem(rep // mask, 2), at)

    tokens_here, width = tokens.shape
    scale = width ** (-0.5)
    half = p_rows // 2
    q_rows = BLOCK - p_rows
    PA, PB = (0, half), (BLOCK - half, half)
    QA, QB, Q = (half, q_rows // 2), (ROWS, q_rows // 2), (half, q_rows)
    H0, H1, ALL = (0, ROWS), (ROWS, ROWS), (0, BLOCK)

    def remote(src, dst, send, recv, device):
        return pltpu.make_async_remote_copy(
            src_ref=src,
            dst_ref=dst,
            send_sem=send,
            recv_sem=recv,
            device_id=device,
            device_id_type=MESH,
        )

    sent = []

    def load(src, dst, i):
        copy = pltpu.make_async_copy(src, dst, local.at[i])
        copy.start()
        return copy

    def cols(c, j):
        return pl.ds(pl.multiple_of(c * CHUNKS * CHUNK + j * CHUNK, CHUNK), CHUNK)

    def half_cols(c):
        return pl.ds(pl.multiple_of(c * CHUNKS * CHUNK, CHUNK), CHUNKS * CHUNK)

    own_start = (z * 2 + x) * BLOCK

    def own_rows(c):
        return pl.ds(pl.multiple_of(own_start + c * ROWS, 64), ROWS)

    w_loads = [
        load(weights.at[:, cols(core, j)], full.at[j, own_rows(core)], j)
        for j in range(CHUNKS)
    ]
    tiles = tokens_here // TILE

    def tile_of(c, i):
        return pl.ds(pl.multiple_of(c * tokens_here + i * TILE, TILE), TILE)

    gain_load = load(gain, gain_v, 2)
    token_base = 8

    @pl.loop(0, tiles)
    def _(i):
        rows = pl.ds(pl.multiple_of(i * TILE, TILE), TILE)
        pltpu.make_async_copy(
            tokens.at[rows], normed.at[tile_of(core, i)], local.at[token_base + i]
        ).start()

    tgt_load = load(target.at[:, half_cols(core)], tgt.at[core], 3)
    own_w_load = load(weights, own_w, 4)
    anchor_load = load(anchor, anchor_v, 5)
    momentum_load = load(momentum, momentum_v, 6)

    barrier = pltpu.get_barrier_semaphore()
    for device in (up, down, mate, sibling, friend):
        pl.semaphore_signal(barrier, inc=1, device_id=device, device_id_type=MESH)
    pl.semaphore_wait(barrier, 5)

    def w_swap(j):
        return remote(
            weights.at[:, cols(other, j)],
            full.at[j, own_rows(core)],
            m_send.at[j],
            m_recv.at[j],
            sibling,
        )

    for j in range(CHUNKS):
        w_swap(j).start()
    tgt_swap = remote(
        target.at[:, half_cols(other)], tgt.at[core], m_send.at[2], m_recv.at[2], sibling
    )
    friend_swap = remote(previous, partner, m_send.at[3], m_recv.at[3], friend)

    def piece(j, zz, xx, part):
        start = pl.multiple_of((zz * 2 + xx) * BLOCK + part[0], 16)
        return full.at[j, pl.ds(start, part[1])]

    def ag_copy(j, i, zz, xx, part, device):
        where = piece(j, zz, xx, part)
        return remote(where, where, ag_send.at[j, i], ag_recv.at[j, i], device)

    def ag_start(j, i, zz, xx, part, device):
        ag_copy(j, i, zz, xx, part, device).start()
        sent.append(lambda: ag_copy(j, i, zz, xx, part, device))

    def ag_wait(j, i, zz, xx, part):
        ag_copy(j, i, zz, xx, part, mate).wait_recv()

    xm = 1 - x

    def gather_own(j):
        w_loads[j].wait()
        pltpu.make_async_copy(
            full.at[j, own_rows(other)], full.at[j, own_rows(other)], m_recv.at[j]
        ).wait()
        ag_start(j, 0, z, x, ALL, mate)
        ag_start(j, 1, z, x, ALL, up)
        ag_start(j, 2, z, x, ALL, down)

    def gather_1(j):
        ag_wait(j, 0, z, xm, ALL)
        ag_start(j, 3, z, xm, PA, up)
        ag_start(j, 6, z, xm, PB, down)
        ag_start(j, 4, z, xm, PB, up)
        ag_start(j, 5, z, xm, PA, down)
        ag_wait(j, 1, z_down, x, ALL)
        ag_start(j, 7, z_down, x, H0, up)
        ag_start(j, 8, z_down, x, Q, mate)
        ag_wait(j, 2, z_up, x, ALL)
        ag_start(j, 9, z_up, x, H1, down)
        ag_start(j, 10, z_up, x, Q, mate)

    def gather_2(j):
        ag_wait(j, 3, z_down, xm, PA)
        ag_start(j, 11, z_down, xm, PA, up)
        ag_wait(j, 6, z_up, xm, PB)
        ag_start(j, 12, z_up, xm, PB, down)

    def gather_3(j):
        ag_wait(j, 7, z_far, x, H0)
        ag_start(j, 13, z_far, x, QA, mate)
        ag_wait(j, 9, z_far, x, H1)
        ag_start(j, 14, z_far, x, QB, mate)

    def gather_4(j):
        ag_wait(j, 4, z_down, xm, PB)
        ag_wait(j, 5, z_up, xm, PA)
        ag_wait(j, 8, z_down, xm, Q)
        ag_wait(j, 10, z_up, xm, Q)
        ag_wait(j, 11, z_far, xm, PA)
        ag_wait(j, 12, z_far, xm, PB)
        ag_wait(j, 13, z_far, xm, QA)
        ag_wait(j, 14, z_far, xm, QB)

    def tile_copy(c, i):
        where = normed.at[tile_of(c, i)]
        return remote(where, where, n_send.at[i], n_recv.at[i], sibling)

    def norm_tile(i):
        where = tile_of(core, i)
        pltpu.make_async_copy(
            normed.at[where], normed.at[where], local.at[token_base + i]
        ).wait()
        for part in range(2):
            rows = pl.ds(
                pl.multiple_of(core * tokens_here + i * TILE + part * (TILE // 2), 64),
                TILE // 2,
            )
            value = normed[rows, :].astype(F32)
            rms = lax.rsqrt(jnp.mean(value * value, axis=-1, keepdims=True) + EPS)
            normed[rows, :] = (value * rms * gain_v[...]).astype(BF16)
        tile_copy(core, i).start()

    steps = tokens_here // STEP

    def values_step(j, s):
        side = jnp.where(s < steps, core, other)
        inner = lax.rem(s, steps) * STEP
        rows = pl.ds(pl.multiple_of(side * tokens_here + inner, STEP), STEP)
        values = jnp.dot(normed[rows, :], full[j], preferred_element_type=F32) * scale
        goal = tgt[
            side, pl.ds(pl.multiple_of(inner, STEP), STEP), j * CHUNK : (j + 1) * CHUNK
        ].astype(F32)
        err[rows, :] = (values - goal).astype(BF16)

    def grad_step(j, s):
        i = s // 2
        dz = jnp.where(i == 0, 2, jnp.where(i == 1, 1, jnp.where(i == 2, 3, 0)))
        block = lax.rem(z + dz, 4) * 2 + jnp.where(lax.rem(s, 2) == 0, 1 - x, x)
        where = pl.ds(pl.multiple_of(block * BLOCK, 128), BLOCK)
        part = lax.dot_general(
            normed[:, where], err[...], (((0,), (0,)), ((), ())), preferred_element_type=F32
        )
        grad[j, s] = part
        grad_half[j, s] = part.astype(BF16)

    def rs_copy(j, i, src, dst, device):
        return remote(src, dst, rs_send.at[j, i], rs_recv.at[j, i], device)

    def rs_start(j, i, src, dst, device):
        rs_copy(j, i, src, dst, device).start()
        is_total, count = src.dtype == F32, src.shape[0]

        def again():
            where = (total if is_total else grad_half.at[j]).at[0, pl.ds(0, count)]
            return rs_copy(j, i, where, where, mate)

        sent.append(again)

    def rs_wait(j, i, dst):
        rs_copy(j, i, dst, dst, mate).wait_recv()

    def out_of(j, s, part):
        return grad_half.at[j, s, pl.ds(*part)]

    far_p = ((0, half), (half, half))
    far_q = (2 * half, q_rows // 2)
    mate_pa, mate_pb = (BLOCK, half), (BLOCK + half, half)

    def near_at(j, d, part):
        return near.at[j, d, pl.ds(*part)]

    def far_at(j, d, part):
        return far.at[j, d, pl.ds(*part)]

    def scatter_q(j, i):
        rs_start(j, i, out_of(j, 2 * i, Q), from_mate.at[j, i], mate)

    def scatter_far(j):
        for c in range(2):
            rs_start(j, 4 + c, out_of(j, c, PA), far_at(j, 0, far_p[c]), up)
            rs_start(j, 6 + c, out_of(j, c, PB), far_at(j, 1, far_p[c]), down)

    def scatter_up(j):
        rs_start(j, 8, out_of(j, 2, PB), near_at(j, 0, mate_pb), up)
        rs_start(j, 9, out_of(j, 3, PB), near_at(j, 0, PB), up)

    def scatter_down(j):
        rs_start(j, 10, out_of(j, 4, PA), near_at(j, 1, mate_pa), down)
        rs_start(j, 11, out_of(j, 5, PA), near_at(j, 1, PA), down)

    def add_and_send(j, s, part, terms, i, dst, device):
        where = pl.ds(*part)
        value = grad[j, s, where, :]
        for term in terms:
            value = value + term[...].astype(F32)
        grad_half[j, s, where, :] = value.astype(BF16)
        rs_start(j, i, out_of(j, s, part), dst, device)

    def relay_p(j):
        for c in range(2):
            rs_wait(j, 4 + c, far_at(j, 0, far_p[c]))
            dst = near_at(j, 0, PA if c else mate_pa)
            add_and_send(j, 2 + c, PA, [far_at(j, 0, far_p[c])], 12 + c, dst, up)
            rs_wait(j, 6 + c, far_at(j, 1, far_p[c]))
            dst = near_at(j, 1, PB if c else mate_pb)
            add_and_send(j, 4 + c, PB, [far_at(j, 1, far_p[c])], 14 + c, dst, down)

    def mate_q(j, i, lower):
        start, count = (0, q_rows // 2) if lower else (q_rows // 2, q_rows // 2)
        return from_mate.at[j, i, pl.ds(start, count)]

    def far_q_send(j):
        rs_wait(j, 0, from_mate.at[j, 0])
        add_and_send(j, 1, QA, [mate_q(j, 0, True)], 16, far_at(j, 0, far_q), up)
        add_and_send(j, 1, QB, [mate_q(j, 0, False)], 17, far_at(j, 1, far_q), down)

    def near_q_up(j):
        rs_wait(j, 1, from_mate.at[j, 1])
        add_and_send(j, 3, QB, [mate_q(j, 1, False)], 18, near_at(j, 0, QB), up)

    def near_q_down(j):
        rs_wait(j, 2, from_mate.at[j, 2])
        add_and_send(j, 5, QA, [mate_q(j, 2, True)], 19, near_at(j, 1, QA), down)

    def relay_q(j):
        rs_wait(j, 16, far_at(j, 0, far_q))
        terms = [mate_q(j, 1, True), far_at(j, 0, far_q)]
        add_and_send(j, 3, QA, terms, 20, near_at(j, 0, QA), up)
        rs_wait(j, 17, far_at(j, 1, far_q))
        terms = [mate_q(j, 2, False), far_at(j, 1, far_q)]
        add_and_send(j, 5, QB, terms, 21, near_at(j, 1, QB), down)

    def mate_send(j):
        rs_wait(j, 12, near_at(j, 0, mate_pa))
        rs_wait(j, 10, near_at(j, 1, mate_pa))
        terms = [near_at(j, 0, mate_pa), near_at(j, 1, mate_pa)]
        add_and_send(j, 6, PA, terms, 22, mate_p.at[j, 0], mate)
        rs_wait(j, 8, near_at(j, 0, mate_pb))
        rs_wait(j, 14, near_at(j, 1, mate_pb))
        terms = [near_at(j, 0, mate_pb), near_at(j, 1, mate_pb)]
        add_and_send(j, 6, PB, terms, 23, mate_p.at[j, 1], mate)

    def finish(j):
        def put(part, terms):
            where = pl.ds(*part)
            value = grad[j, 7, where, :]
            for term in terms:
                value = value + term[...].astype(F32)
            total[j, where, :] = value

        rs_wait(j, 3, from_mate.at[j, 3])
        rs_wait(j, 13, near_at(j, 0, PA))
        rs_wait(j, 11, near_at(j, 1, PA))
        rs_wait(j, 22, mate_p.at[j, 0])
        put(PA, [near_at(j, 0, PA), near_at(j, 1, PA), mate_p.at[j, 0]])
        rs_wait(j, 9, near_at(j, 0, PB))
        rs_wait(j, 15, near_at(j, 1, PB))
        rs_wait(j, 23, mate_p.at[j, 1])
        put(PB, [near_at(j, 0, PB), near_at(j, 1, PB), mate_p.at[j, 1]])
        rs_wait(j, 20, near_at(j, 0, QA))
        rs_wait(j, 19, near_at(j, 1, QA))
        put(QA, [near_at(j, 0, QA), near_at(j, 1, QA), mate_q(j, 3, True)])
        rs_wait(j, 18, near_at(j, 0, QB))
        rs_wait(j, 21, near_at(j, 1, QB))
        put(QB, [near_at(j, 0, QB), near_at(j, 1, QB), mate_q(j, 3, False)])
        theirs = pl.ds(pl.multiple_of(other * ROWS, 64), ROWS)
        rs_start(j, 24, total.at[j, theirs], swapped.at[j], sibling)

    def update(columns, gradient):
        fast = own_w[:, columns].astype(F32) - INNER_RATE * (gradient * scale)
        mixed = 0.5 * fast + 0.5 * partner[:, columns].astype(F32)
        base = anchor_v[:, columns]
        moment = SLOW_BETA * momentum_v[:, columns] + (base - mixed) / INNER_RATE
        new_momentum[:, columns] = moment
        new_anchor[:, columns] = base - OUTER_RATE * INNER_RATE * moment

    def update_own(j):
        mine = pl.ds(pl.multiple_of(core * ROWS, 64), ROWS)
        update(cols(core, j), total[j, mine, :])

    def update_other(j):
        rs_wait(j, 24, swapped.at[j])
        update(cols(other, j), swapped[j])

    gather_own(0)
    gain_load.wait()

    @pl.loop(0, tiles)
    def _(i):
        norm_tile(i)

    tgt_swap.start()
    gather_1(0)
    gather_2(0)
    gather_own(1)
    friend_swap.start()
    gather_3(0)
    gather_4(0)
    tgt_load.wait()

    @pl.loop(0, steps)
    def _(s):
        values_step(0, s)

    gather_1(1)
    pltpu.make_async_copy(tgt.at[other], tgt.at[other], m_recv.at[2]).wait()

    @pl.loop(0, tiles)
    def _(i):
        tile_copy(other, i).wait_recv()

    @pl.loop(steps, 2 * steps)
    def _(s):
        values_step(0, s)

    gather_2(1)

    @pl.loop(0, 8)
    def _(s):
        grad_step(0, s)

        @pl.when(s == 3)
        def _():
            gather_3(1)

    def scatter_begin(j):
        scatter_far(j)
        scatter_q(j, 0)
        scatter_q(j, 1)
        scatter_up(j)
        scatter_q(j, 2)
        scatter_down(j)
        scatter_q(j, 3)

    scatter_begin(0)
    gather_4(1)

    @pl.loop(0, 2 * steps)
    def _(s):
        values_step(1, s)

    relay_p(0)
    far_q_send(0)

    @pl.loop(0, 8)
    def _(s):
        grad_step(1, s)

        @pl.when(s == 3)
        def _():
            near_q_up(0)
            near_q_down(0)

    scatter_begin(1)
    relay_q(0)
    mate_send(0)
    friend_swap.wait_recv()
    own_w_load.wait()
    anchor_load.wait()
    momentum_load.wait()
    relay_p(1)
    far_q_send(1)
    finish(0)
    near_q_up(1)
    near_q_down(1)
    update_own(0)
    mate_send(1)
    relay_q(1)
    update_other(0)
    finish(1)
    update_own(1)
    update_other(1)

    for j in range(CHUNKS):
        w_swap(j).wait_send()
    tgt_swap.wait_send()
    friend_swap.wait_send()

    @pl.loop(0, tiles)
    def _(i):
        tile_copy(core, i).wait_send()

    for copy in sent:
        copy().wait_send()


def run(mask, p_rows, collective_id, tokens, target, gain, weights, previous, anchor, momentum):
    rows, width = tokens.shape
    kv = target.shape[1]
    half, q_rows = p_rows // 2, BLOCK - p_rows
    anywhere = pl.BlockSpec(memory_space=pl.ANY)
    here = pl.BlockSpec(memory_space=pltpu.VMEM)
    vmem, dma = pltpu.VMEM, pltpu.SemaphoreType.DMA
    side = CHUNKS * CHUNK
    return pl.pallas_call(
        functools.partial(kernel, mask, p_rows),
        out_shape=(
            jax.ShapeDtypeStruct((ROWS, kv), F32),
            jax.ShapeDtypeStruct((ROWS, kv), F32),
        ),
        in_specs=[anywhere] * 7,
        out_specs=(here, here),
        scratch_shapes=[
            vmem((2 * rows, width), BF16),
            vmem((CHUNKS, width, CHUNK), BF16),
            vmem((CHUNKS, 8, BLOCK, CHUNK), F32),
            vmem((CHUNKS, 8, BLOCK, CHUNK), BF16),
            vmem((2, rows, side), BF16),
            vmem((2 * rows, CHUNK), BF16),
            vmem((CHUNKS, 4, q_rows, CHUNK), BF16),
            vmem((CHUNKS, 2, p_rows + q_rows // 2, CHUNK), BF16),
            vmem((CHUNKS, 2, BLOCK + p_rows, CHUNK), BF16),
            vmem((CHUNKS, 2, half, CHUNK), BF16),
            vmem((CHUNKS, BLOCK, CHUNK), F32),
            vmem((CHUNKS, ROWS, CHUNK), F32),
            vmem((ROWS, kv), BF16),
            vmem((ROWS, kv), BF16),
            vmem((ROWS, kv), F32),
            vmem((ROWS, kv), F32),
            vmem((1, width), F32),
            dma((CHUNKS, N_AG)),
            dma((CHUNKS, N_AG)),
            dma((CHUNKS, N_RS)),
            dma((CHUNKS, N_RS)),
            dma((rows // TILE,)),
            dma((rows // TILE,)),
            dma((4,)),
            dma((4,)),
            dma((8 + rows // TILE,)),
        ],
        compiler_params=pltpu.CompilerParams(
            collective_id=collective_id,
            has_side_effects=True,
            vmem_limit_bytes=63 << 20,
        ),
    )(tokens, target, gain, weights, previous, anchor, momentum)


def shards(step_bit, tokens, target, norm_gain, weights, previous, anchor, momentum):
    bit_count = lax.axis_size("rep").bit_length() - 1
    chosen_bit = jnp.remainder(step_bit, jnp.int32(bit_count))
    branches = [
        functools.partial(run, 2**bit, 416 if bit == 0 else 352, bit)
        for bit in range(bit_count)
    ]
    moment_new, anchor_new = lax.switch(
        chosen_bit,
        branches,
        tokens[0],
        target[0],
        norm_gain[None],
        weights[0],
        previous[0],
        anchor[0],
        momentum[0],
    )
    return (moment_new[None], anchor_new[None])


def solution(mesh):
    placed = (
        P(),
        P("rep", "fsdp", None),
        P("rep", "fsdp", None),
        P(),
        P("rep", "fsdp", None),
        P("rep", "fsdp", None),
        P("rep", "fsdp", None),
        P("rep", "fsdp", None),
    )
    return jax.shard_map(
        shards,
        mesh=mesh,
        in_specs=placed,
        out_specs=(P("rep", "fsdp", None), P("rep", "fsdp", None)),
        check_vma=False,
    )
```

```python
import functools

import jax
import jax.numpy as jnp
from jax import lax
from jax.experimental import pallas as pl
from jax.experimental.pallas import tpu as pltpu
from jax.sharding import PartitionSpec as P

EPS = 1e-06
INNER_RATE = 0.05
OUTER_RATE = 1.0
SLOW_BETA = 0.6

MESH = pl.DeviceIdType.MESH
BF16 = jnp.bfloat16
F32 = jnp.float32

ROWS = 320
BLOCK = 2 * ROWS
CHUNK = 256
CHUNKS = 2
FRIEND_PARTS = 4
TILE = 128
STEP = 512
N_AG = 18
N_RS = 26


def kernel(
    mask,
    p_rows,
    tokens,
    target,
    gain,
    weights,
    previous,
    anchor,
    momentum,
    new_momentum,
    new_anchor,
    normed,
    full,
    grad,
    grad_half,
    tgt,
    err,
    from_mate,
    far,
    near,
    mate_p,
    total,
    swapped,
    own_w,
    partner,
    anchor_v,
    momentum_v,
    gain_v,
    ag_send,
    ag_recv,
    rs_send,
    rs_recv,
    n_send,
    n_recv,
    m_send,
    m_recv,
    local,
):
    rep = lax.axis_index("rep")
    at = lax.axis_index("fsdp")
    core = lax.rem(at, 2)
    other = 1 - core
    x = lax.rem(at // 2, 2)
    z = at // 4
    z_up, z_down, z_far = lax.rem(z + 1, 4), lax.rem(z + 3, 4), lax.rem(z + 2, 4)
    up, up_other = [(rep, z_up * 4 + x * 2 + c) for c in (core, other)]
    down, down_other = [(rep, z_down * 4 + x * 2 + c) for c in (core, other)]
    mate, mate_other = [(rep, z * 4 + (1 - x) * 2 + c) for c in (core, other)]
    sibling = (rep, z * 4 + x * 2 + other)
    friend = (rep + mask - 2 * mask * lax.rem(rep // mask, 2), at)

    tokens_here, width = tokens.shape
    scale = width ** (-0.5)
    half = p_rows // 2
    q_rows = BLOCK - p_rows
    PA, PB = (0, half), (BLOCK - half, half)
    QA, QB, Q = (half, q_rows // 2), (ROWS, q_rows // 2), (half, q_rows)
    H0, H1, ALL = (0, ROWS), (ROWS, ROWS), (0, BLOCK)

    def remote(src, dst, send, recv, device):
        return pltpu.make_async_remote_copy(
            src_ref=src,
            dst_ref=dst,
            send_sem=send,
            recv_sem=recv,
            device_id=device,
            device_id_type=MESH,
        )

    sent = []

    def load(src, dst, i):
        copy = pltpu.make_async_copy(src, dst, local.at[i])
        copy.start()
        return copy

    def cols(c, j):
        return pl.ds(pl.multiple_of(c * CHUNKS * CHUNK + j * CHUNK, CHUNK), CHUNK)

    def half_cols(c):
        return pl.ds(pl.multiple_of(c * CHUNKS * CHUNK, CHUNK), CHUNKS * CHUNK)

    own_base = (z * 2 + x) * BLOCK

    def own_rows(c):
        return pl.ds(pl.multiple_of(own_base + c * ROWS, 64), ROWS)

    w_loads = [
        load(weights.at[:, cols(core, j)], full.at[j, own_rows(core)], j)
        for j in range(CHUNKS)
    ]
    tiles = tokens_here // TILE

    def tile_of(c, i):
        return pl.ds(pl.multiple_of(c * tokens_here + i * TILE, TILE), TILE)

    gain_load = load(gain, gain_v, 2)
    token_base = 8

    @pl.loop(0, tiles)
    def _(i):
        rows = pl.ds(pl.multiple_of(i * TILE, TILE), TILE)
        pltpu.make_async_copy(
            tokens.at[rows], normed.at[tile_of(core, i)], local.at[token_base + i]
        ).start()

    tgt_load = load(target.at[:, half_cols(core)], tgt.at[core], 3)
    own_w_load = load(weights, own_w, 4)
    anchor_load = load(anchor, anchor_v, 5)
    momentum_load = load(momentum, momentum_v, 6)

    barrier = pltpu.get_barrier_semaphore()
    everyone = (up, up_other, down, down_other, mate, mate_other, sibling, friend)
    for device in everyone:
        pl.semaphore_signal(barrier, inc=1, device_id=device, device_id_type=MESH)
    pl.semaphore_wait(barrier, len(everyone))

    def w_swap(j):
        return remote(
            weights.at[:, cols(other, j)],
            full.at[j, own_rows(core)],
            m_send.at[j],
            m_recv.at[j],
            sibling,
        )
    tgt_swap = remote(
        target.at[:, half_cols(other)], tgt.at[core], m_send.at[2], m_recv.at[2], sibling
    )
    friend_rows = ROWS // FRIEND_PARTS

    def friend_swap(i):
        where = pl.ds(i * friend_rows, friend_rows)
        return remote(
            previous.at[where], partner.at[where], m_send.at[3 + i], m_recv.at[3 + i], friend
        )

    def piece(j, zz, xx, part):
        start = pl.multiple_of((zz * 2 + xx) * BLOCK + part[0], 16)
        return full.at[j, pl.ds(start, part[1])]

    def ag_copy(j, i, zz, xx, part, device):
        where = piece(j, zz, xx, part)
        return remote(where, where, ag_send.at[j, i], ag_recv.at[j, i], device)

    def ag_start(j, i, zz, xx, part, device):
        ag_copy(j, i, zz, xx, part, device).start()
        sent.append(lambda: ag_copy(j, i, zz, xx, part, device))

    def ag_wait(j, i, zz, xx, part):
        ag_copy(j, i, zz, xx, part, mate).wait_recv()

    xm = 1 - x

    def own_copy(j, i, c, device):
        return remote(
            weights.at[:, cols(c, j)],
            full.at[j, own_rows(core)],
            ag_send.at[j, i + jnp.where(c == core, 0, 1)],
            ag_recv.at[j, i + core],
            device,
        )

    def own_start(j, i, same, cross):
        for c, device in ((core, same), (other, cross)):
            own_copy(j, i, c, device).start()
            sent.append(lambda c=c, device=device: own_copy(j, i, c, device))

    def own_wait(j, i, zz, xx, h):
        where = piece(j, zz, xx, (H0, H1)[h])
        remote(where, where, ag_send.at[j, i], ag_recv.at[j, i + h], mate).wait_recv()

    def gather_own_z(j):
        own_start(j, 2, up, up_other)
        own_start(j, 4, down, down_other)

    def gather_own_x(j):
        own_start(j, 0, mate, mate_other)
        w_swap(j).start()

    def gather_1(j):
        own_wait(j, 0, z, xm, 0)
        ag_start(j, 6, z, xm, PA, up)
        ag_start(j, 8, z, xm, PA, down)
        own_wait(j, 0, z, xm, 1)
        ag_start(j, 9, z, xm, PB, down)
        ag_start(j, 7, z, xm, PB, up)
        own_wait(j, 2, z_down, x, 0)
        ag_start(j, 10, z_down, x, H0, up)
        own_wait(j, 4, z_up, x, 1)
        ag_start(j, 12, z_up, x, H1, down)
        own_wait(j, 2, z_down, x, 1)
        ag_start(j, 11, z_down, x, Q, mate)
        own_wait(j, 4, z_up, x, 0)
        ag_start(j, 13, z_up, x, Q, mate)

    def gather_2(j):
        ag_wait(j, 6, z_down, xm, PA)
        ag_start(j, 14, z_down, xm, PA, up)
        ag_wait(j, 9, z_up, xm, PB)
        ag_start(j, 15, z_up, xm, PB, down)

    def gather_3(j):
        ag_wait(j, 10, z_far, x, H0)
        ag_start(j, 16, z_far, x, QA, mate)
        ag_wait(j, 12, z_far, x, H1)
        ag_start(j, 17, z_far, x, QB, mate)

    def gather_4(j):
        w_loads[j].wait()
        w_swap(j).wait_recv()
        ag_wait(j, 7, z_down, xm, PB)
        ag_wait(j, 8, z_up, xm, PA)
        ag_wait(j, 11, z_down, xm, Q)
        ag_wait(j, 13, z_up, xm, Q)
        ag_wait(j, 14, z_far, xm, PA)
        ag_wait(j, 15, z_far, xm, PB)
        ag_wait(j, 16, z_far, xm, QA)
        ag_wait(j, 17, z_far, xm, QB)

    def tile_copy(c, i):
        where = normed.at[tile_of(c, i)]
        return remote(where, where, n_send.at[i], n_recv.at[i], sibling)

    def norm_tile(i):
        where = tile_of(core, i)
        pltpu.make_async_copy(
            normed.at[where], normed.at[where], local.at[token_base + i]
        ).wait()
        for part in range(2):
            rows = pl.ds(
                pl.multiple_of(core * tokens_here + i * TILE + part * (TILE // 2), 64),
                TILE // 2,
            )
            value = normed[rows, :].astype(F32)
            rms = lax.rsqrt(jnp.mean(value * value, axis=-1, keepdims=True) + EPS)
            normed[rows, :] = (value * rms * gain_v[...]).astype(BF16)
        tile_copy(core, i).start()

    steps = tokens_here // STEP

    def values_step(j, s):
        side = jnp.where(s < steps, core, other)
        inner = lax.rem(s, steps) * STEP
        rows = pl.ds(pl.multiple_of(side * tokens_here + inner, STEP), STEP)
        values = jnp.dot(normed[rows, :], full[j], preferred_element_type=F32) * scale
        goal = tgt[
            side, pl.ds(pl.multiple_of(inner, STEP), STEP), j * CHUNK : (j + 1) * CHUNK
        ].astype(F32)
        err[rows, :] = (values - goal).astype(BF16)

    def grad_step(j, s):
        i = s // 2
        dz = jnp.where(i == 0, 2, jnp.where(i == 1, 1, jnp.where(i == 2, 3, 0)))
        block = lax.rem(z + dz, 4) * 2 + jnp.where(lax.rem(s, 2) == 0, 1 - x, x)
        where = pl.ds(pl.multiple_of(block * BLOCK, 128), BLOCK)
        part = lax.dot_general(
            normed[:, where], err[...], (((0,), (0,)), ((), ())), preferred_element_type=F32
        )
        grad[j, s] = part
        grad_half[j, s] = part.astype(BF16)

    def rs_copy(j, i, src, dst, device):
        return remote(src, dst, rs_send.at[j, i], rs_recv.at[j, i], device)

    def rs_start(j, i, src, dst, device):
        rs_copy(j, i, src, dst, device).start()
        is_total, count = src.dtype == F32, src.shape[0]

        def again():
            where = (total if is_total else grad_half.at[j]).at[0, pl.ds(0, count)]
            return rs_copy(j, i, where, where, mate)

        sent.append(again)

    def rs_wait(j, i, dst):
        rs_copy(j, i, dst, dst, mate).wait_recv()

    def out_of(j, s, part):
        return grad_half.at[j, s, pl.ds(*part)]

    far_p = ((0, half), (half, half))
    far_q = (2 * half, q_rows // 2)
    mate_pa, mate_pb = (BLOCK, half), (BLOCK + half, half)

    def near_at(j, d, part):
        return near.at[j, d, pl.ds(*part)]

    def far_at(j, d, part):
        return far.at[j, d, pl.ds(*part)]

    def scatter_q(j, i):
        rs_start(j, i, out_of(j, 2 * i, Q), from_mate.at[j, i], mate)

    def scatter_far(j):
        for c in range(2):
            rs_start(j, 4 + c, out_of(j, c, PA), far_at(j, 0, far_p[c]), up)
            rs_start(j, 6 + c, out_of(j, c, PB), far_at(j, 1, far_p[c]), down)

    def scatter_up(j):
        rs_start(j, 8, out_of(j, 2, PB), near_at(j, 0, mate_pb), up)
        rs_start(j, 9, out_of(j, 3, PB), near_at(j, 0, PB), up)

    def scatter_down(j):
        rs_start(j, 10, out_of(j, 4, PA), near_at(j, 1, mate_pa), down)
        rs_start(j, 11, out_of(j, 5, PA), near_at(j, 1, PA), down)

    def add_and_send(j, s, part, terms, i, dst, device):
        where = pl.ds(*part)
        value = grad[j, s, where, :]
        for term in terms:
            value = value + term[...].astype(F32)
        grad_half[j, s, where, :] = value.astype(BF16)
        rs_start(j, i, out_of(j, s, part), dst, device)

    def relay_p(j):
        for c in range(2):
            rs_wait(j, 4 + c, far_at(j, 0, far_p[c]))
            dst = near_at(j, 0, PA if c else mate_pa)
            add_and_send(j, 2 + c, PA, [far_at(j, 0, far_p[c])], 12 + c, dst, up)
            rs_wait(j, 6 + c, far_at(j, 1, far_p[c]))
            dst = near_at(j, 1, PB if c else mate_pb)
            add_and_send(j, 4 + c, PB, [far_at(j, 1, far_p[c])], 14 + c, dst, down)

    def mate_q(j, i, lower):
        start, count = (0, q_rows // 2) if lower else (q_rows // 2, q_rows // 2)
        return from_mate.at[j, i, pl.ds(start, count)]

    def far_q_send(j):
        rs_wait(j, 0, from_mate.at[j, 0])
        add_and_send(j, 1, QA, [mate_q(j, 0, True)], 16, far_at(j, 0, far_q), up)
        add_and_send(j, 1, QB, [mate_q(j, 0, False)], 17, far_at(j, 1, far_q), down)

    def near_q_up(j):
        rs_wait(j, 1, from_mate.at[j, 1])
        add_and_send(j, 3, QB, [mate_q(j, 1, False)], 18, near_at(j, 0, QB), up)

    def near_q_down(j):
        rs_wait(j, 2, from_mate.at[j, 2])
        add_and_send(j, 5, QA, [mate_q(j, 2, True)], 19, near_at(j, 1, QA), down)

    def relay_q(j):
        rs_wait(j, 16, far_at(j, 0, far_q))
        terms = [mate_q(j, 1, True), far_at(j, 0, far_q)]
        add_and_send(j, 3, QA, terms, 20, near_at(j, 0, QA), up)
        rs_wait(j, 17, far_at(j, 1, far_q))
        terms = [mate_q(j, 2, False), far_at(j, 1, far_q)]
        add_and_send(j, 5, QB, terms, 21, near_at(j, 1, QB), down)

    def mate_send(j):
        rs_wait(j, 12, near_at(j, 0, mate_pa))
        rs_wait(j, 10, near_at(j, 1, mate_pa))
        terms = [near_at(j, 0, mate_pa), near_at(j, 1, mate_pa)]
        add_and_send(j, 6, PA, terms, 22, mate_p.at[j, 0], mate)
        rs_wait(j, 8, near_at(j, 0, mate_pb))
        rs_wait(j, 14, near_at(j, 1, mate_pb))
        terms = [near_at(j, 0, mate_pb), near_at(j, 1, mate_pb)]
        add_and_send(j, 6, PB, terms, 23, mate_p.at[j, 1], mate)

    def finish(j):
        def put(part, terms):
            where = pl.ds(*part)
            value = grad[j, 7, where, :]
            for term in terms:
                value = value + term[...].astype(F32)
            total[j, where, :] = value

        rs_wait(j, 3, from_mate.at[j, 3])
        rs_wait(j, 13, near_at(j, 0, PA))
        rs_wait(j, 11, near_at(j, 1, PA))
        rs_wait(j, 22, mate_p.at[j, 0])
        put(PA, [near_at(j, 0, PA), near_at(j, 1, PA), mate_p.at[j, 0]])
        rs_wait(j, 9, near_at(j, 0, PB))
        rs_wait(j, 15, near_at(j, 1, PB))
        rs_wait(j, 23, mate_p.at[j, 1])
        put(PB, [near_at(j, 0, PB), near_at(j, 1, PB), mate_p.at[j, 1]])
        rs_wait(j, 20, near_at(j, 0, QA))
        rs_wait(j, 19, near_at(j, 1, QA))
        put(QA, [near_at(j, 0, QA), near_at(j, 1, QA), mate_q(j, 3, True)])
        rs_wait(j, 18, near_at(j, 0, QB))
        rs_wait(j, 21, near_at(j, 1, QB))
        put(QB, [near_at(j, 0, QB), near_at(j, 1, QB), mate_q(j, 3, False)])
        theirs = pl.ds(pl.multiple_of(other * ROWS, 64), ROWS)
        rs_start(j, 24, total.at[j, theirs], swapped.at[j], sibling)

    def update(columns, gradient):
        fast = own_w[:, columns].astype(F32) - INNER_RATE * (gradient * scale)
        mixed = 0.5 * fast + 0.5 * partner[:, columns].astype(F32)
        base = anchor_v[:, columns]
        moment = SLOW_BETA * momentum_v[:, columns] + (base - mixed) / INNER_RATE
        new_momentum[:, columns] = moment
        new_anchor[:, columns] = base - OUTER_RATE * INNER_RATE * moment

    def update_own(j):
        mine = pl.ds(pl.multiple_of(core * ROWS, 64), ROWS)
        update(cols(core, j), total[j, mine, :])

    def update_other(j):
        rs_wait(j, 24, swapped.at[j])
        update(cols(other, j), swapped[j])

    def when(s, step, *todo):
        @pl.when(s == step)
        def _():
            for do in todo:
                do()

    def friend_part(i):
        if mask == 1:
            friend_swap(i).start()

    gather_own_x(0)
    gather_own_z(0)
    if mask != 1:
        for i in range(FRIEND_PARTS):
            friend_swap(i).start()
    friend_part(0)
    tgt_swap.start()
    gain_load.wait()

    @pl.loop(0, tiles)
    def _(i):
        norm_tile(i)

    gather_1(0)
    gather_2(0)
    gather_own_z(1)
    gather_3(0)
    gather_own_x(1)
    friend_part(1)
    gather_4(0)
    tgt_load.wait()

    @pl.loop(0, steps)
    def _(s):
        values_step(0, s)

    gather_1(1)
    tgt_swap.wait_recv()

    @pl.loop(0, tiles)
    def _(i):
        tile_copy(other, i).wait_recv()

    @pl.loop(steps, 2 * steps)
    def _(s):
        values_step(0, s)

    gather_2(1)

    @pl.loop(0, 8)
    def _(s):
        grad_step(0, s)
        when(s, 1, lambda: scatter_far(0))
        when(
            s,
            3,
            lambda: gather_3(1),
            lambda: scatter_q(0, 0),
            lambda: scatter_up(0),
            lambda: scatter_q(0, 1),
        )
        when(s, 5, lambda: scatter_q(0, 2), lambda: scatter_down(0))
        when(s, 7, lambda: scatter_q(0, 3), lambda: friend_part(2))

    gather_4(1)

    @pl.loop(0, 2 * steps)
    def _(s):
        values_step(1, s)
        when(s, 0, lambda: relay_p(0))
        when(s, 1, lambda: far_q_send(0))
        when(s, 3, lambda: near_q_up(0))

    @pl.loop(0, 8)
    def _(s):
        grad_step(1, s)
        when(s, 1, lambda: scatter_far(1))
        when(s, 2, lambda: mate_send(0), lambda: near_q_down(0))
        when(s, 3, lambda: scatter_up(1), lambda: scatter_q(1, 0), lambda: scatter_q(1, 1))
        when(s, 4, lambda: relay_q(0))
        when(s, 5, lambda: scatter_down(1), lambda: scatter_q(1, 2))
        when(s, 7, lambda: scatter_q(1, 3), lambda: friend_part(3))

    own_w_load.wait()
    anchor_load.wait()
    momentum_load.wait()
    if mask != 1:
        for i in range(FRIEND_PARTS):
            friend_swap(i).wait_recv()
    relay_p(1)
    finish(0)
    far_q_send(1)
    near_q_up(1)
    mate_send(1)
    near_q_down(1)
    relay_q(1)
    if mask == 1:
        for i in range(FRIEND_PARTS):
            friend_swap(i).wait_recv()
    update_own(0)
    update_other(0)
    finish(1)
    update_own(1)
    update_other(1)

    for j in range(CHUNKS):
        w_swap(j).wait_send()
    tgt_swap.wait_send()
    for i in range(FRIEND_PARTS):
        friend_swap(i).wait_send()

    @pl.loop(0, tiles)
    def _(i):
        tile_copy(core, i).wait_send()

    for copy in sent:
        copy().wait_send()


def run(mask, p_rows, collective_id, tokens, target, gain, weights, previous, anchor, momentum):
    rows, width = tokens.shape
    kv = target.shape[1]
    half, q_rows = p_rows // 2, BLOCK - p_rows
    anywhere = pl.BlockSpec(memory_space=pl.ANY)
    here = pl.BlockSpec(memory_space=pltpu.VMEM)
    vmem, dma = pltpu.VMEM, pltpu.SemaphoreType.DMA
    side = CHUNKS * CHUNK
    return pl.pallas_call(
        functools.partial(kernel, mask, p_rows),
        out_shape=(
            jax.ShapeDtypeStruct((ROWS, kv), F32),
            jax.ShapeDtypeStruct((ROWS, kv), F32),
        ),
        in_specs=[anywhere] * 7,
        out_specs=(here, here),
        scratch_shapes=[
            vmem((2 * rows, width), BF16),
            vmem((CHUNKS, width, CHUNK), BF16),
            vmem((CHUNKS, 8, BLOCK, CHUNK), F32),
            vmem((CHUNKS, 8, BLOCK, CHUNK), BF16),
            vmem((2, rows, side), BF16),
            vmem((2 * rows, CHUNK), BF16),
            vmem((CHUNKS, 4, q_rows, CHUNK), BF16),
            vmem((CHUNKS, 2, p_rows + q_rows // 2, CHUNK), BF16),
            vmem((CHUNKS, 2, BLOCK + p_rows, CHUNK), BF16),
            vmem((CHUNKS, 2, half, CHUNK), BF16),
            vmem((CHUNKS, BLOCK, CHUNK), F32),
            vmem((CHUNKS, ROWS, CHUNK), F32),
            vmem((ROWS, kv), BF16),
            vmem((ROWS, kv), BF16),
            vmem((ROWS, kv), F32),
            vmem((ROWS, kv), F32),
            vmem((1, width), F32),
            dma((CHUNKS, N_AG)),
            dma((CHUNKS, N_AG)),
            dma((CHUNKS, N_RS)),
            dma((CHUNKS, N_RS)),
            dma((rows // TILE,)),
            dma((rows // TILE,)),
            dma((3 + FRIEND_PARTS,)),
            dma((3 + FRIEND_PARTS,)),
            dma((8 + rows // TILE,)),
        ],
        compiler_params=pltpu.CompilerParams(
            collective_id=collective_id,
            has_side_effects=True,
            vmem_limit_bytes=63 << 20,
        ),
    )(tokens, target, gain, weights, previous, anchor, momentum)


def shards(step_bit, tokens, target, norm_gain, weights, previous, anchor, momentum):
    bit_count = lax.axis_size("rep").bit_length() - 1
    chosen_bit = jnp.remainder(step_bit, jnp.int32(bit_count))
    branches = [
        functools.partial(run, 2**bit, 416 if bit == 0 else 352, bit)
        for bit in range(bit_count)
    ]
    moment_new, anchor_new = lax.switch(
        chosen_bit,
        branches,
        tokens[0],
        target[0],
        norm_gain[None],
        weights[0],
        previous[0],
        anchor[0],
        momentum[0],
    )
    return (moment_new[None], anchor_new[None])


def solution(mesh):
    placed = (
        P(),
        P("rep", "fsdp", None),
        P("rep", "fsdp", None),
        P(),
        P("rep", "fsdp", None),
        P("rep", "fsdp", None),
        P("rep", "fsdp", None),
        P("rep", "fsdp", None),
    )
    return jax.shard_map(
        shards,
        mesh=mesh,
        in_specs=placed,
        out_specs=(P("rep", "fsdp", None), P("rep", "fsdp", None)),
        check_vma=False,
    )
```

```python
import functools

import jax
import jax.numpy as jnp
from jax import lax
from jax.experimental import pallas as pl
from jax.experimental.pallas import tpu as pltpu
from jax.sharding import PartitionSpec as P

EPS = 1e-06
INNER_RATE = 0.05
OUTER_RATE = 1.0
SLOW_BETA = 0.6

MESH = pl.DeviceIdType.MESH
BF16 = jnp.bfloat16
F32 = jnp.float32

ROWS = 320
BLOCK = 2 * ROWS
CHUNK = 256
CHUNKS = 2
FRIEND_PARTS = 4
TILE = 128
STEP = 512
N_AG = 20
N_RS = 26


def kernel(
    mask,
    p_rows,
    tokens,
    target,
    gain,
    weights,
    previous,
    anchor,
    momentum,
    new_momentum,
    new_anchor,
    normed,
    full,
    grad,
    grad_half,
    tgt,
    err,
    from_mate,
    far,
    near,
    mate_p,
    total,
    swapped,
    own_w,
    partner,
    anchor_v,
    momentum_v,
    gain_v,
    ag_send,
    ag_recv,
    rs_send,
    rs_recv,
    n_send,
    n_recv,
    m_send,
    m_recv,
    local,
):
    rep = lax.axis_index("rep")
    at = lax.axis_index("fsdp")
    core = lax.rem(at, 2)
    other = 1 - core
    x = lax.rem(at // 2, 2)
    z = at // 4
    z_up, z_down, z_far = lax.rem(z + 1, 4), lax.rem(z + 3, 4), lax.rem(z + 2, 4)
    up, up_other = [(rep, z_up * 4 + x * 2 + c) for c in (core, other)]
    down, down_other = [(rep, z_down * 4 + x * 2 + c) for c in (core, other)]
    mate, mate_other = [(rep, z * 4 + (1 - x) * 2 + c) for c in (core, other)]
    sibling = (rep, z * 4 + x * 2 + other)
    friend = (rep + mask - 2 * mask * lax.rem(rep // mask, 2), at)

    tokens_here, width = tokens.shape
    scale = width ** (-0.5)
    half = p_rows // 2
    q_rows = BLOCK - p_rows
    PA, PB = (0, half), (BLOCK - half, half)
    QA, QB, Q = (half, q_rows // 2), (ROWS, q_rows // 2), (half, q_rows)

    def remote(src, dst, send, recv, device):
        return pltpu.make_async_remote_copy(
            src_ref=src,
            dst_ref=dst,
            send_sem=send,
            recv_sem=recv,
            device_id=device,
            device_id_type=MESH,
        )

    sent = []

    barrier = pltpu.get_barrier_semaphore()
    everyone = (up, up_other, down, down_other, mate, mate_other, sibling, friend)
    for device in everyone:
        pl.semaphore_signal(barrier, inc=1, device_id=device, device_id_type=MESH)

    def load(src, dst, i):
        copy = pltpu.make_async_copy(src, dst, local.at[i])
        copy.start()
        return copy

    def cols(c, j):
        return pl.ds(pl.multiple_of(c * CHUNKS * CHUNK + j * CHUNK, CHUNK), CHUNK)

    def half_cols(c):
        return pl.ds(pl.multiple_of(c * CHUNKS * CHUNK, CHUNK), CHUNKS * CHUNK)

    own_base = (z * 2 + x) * BLOCK

    def own_rows(c):
        return pl.ds(pl.multiple_of(own_base + c * ROWS, 64), ROWS)

    w_loads = [
        load(weights.at[:, cols(core, j)], full.at[j, own_rows(core)], j)
        for j in range(CHUNKS)
    ]
    tiles = tokens_here // TILE

    def tile_of(c, i):
        return pl.ds(pl.multiple_of(c * tokens_here + i * TILE, TILE), TILE)

    gain_load = load(gain, gain_v, 2)
    token_base = 8

    @pl.loop(0, tiles)
    def _(i):
        rows = pl.ds(pl.multiple_of(i * TILE, TILE), TILE)
        pltpu.make_async_copy(
            tokens.at[rows], normed.at[tile_of(core, i)], local.at[token_base + i]
        ).start()

    tgt_load = load(target.at[:, half_cols(core)], tgt.at[core], 3)
    own_w_load = load(weights, own_w, 4)
    anchor_load = load(anchor, anchor_v, 5)
    momentum_load = load(momentum, momentum_v, 6)

    pl.semaphore_wait(barrier, len(everyone))

    def w_swap(j):
        return remote(
            weights.at[:, cols(other, j)],
            full.at[j, own_rows(core)],
            m_send.at[j],
            m_recv.at[j],
            sibling,
        )
    tgt_swap = remote(
        target.at[:, half_cols(other)], tgt.at[core], m_send.at[2], m_recv.at[2], sibling
    )
    friend_rows = ROWS // FRIEND_PARTS

    def friend_swap(i):
        where = pl.ds(i * friend_rows, friend_rows)
        return remote(
            previous.at[where], partner.at[where], m_send.at[3 + i], m_recv.at[3 + i], friend
        )

    def piece(j, zz, xx, part):
        start = pl.multiple_of((zz * 2 + xx) * BLOCK + part[0], 16)
        return full.at[j, pl.ds(start, part[1])]

    def ag_copy(j, i, zz, xx, part, device):
        where = piece(j, zz, xx, part)
        return remote(where, where, ag_send.at[j, i], ag_recv.at[j, i], device)

    def ag_start(j, i, zz, xx, part, device):
        ag_copy(j, i, zz, xx, part, device).start()
        sent.append(lambda: ag_copy(j, i, z, x, (0, part[1]), mate))

    def ag_wait(j, i, zz, xx, part):
        ag_copy(j, i, zz, xx, part, mate).wait_recv()

    xm = 1 - x

    def own_copy(j, i, c, device):
        return remote(
            weights.at[:, cols(c, j)],
            full.at[j, own_rows(core)],
            ag_send.at[j, i + jnp.where(c == core, 0, 1)],
            ag_recv.at[j, i + core],
            device,
        )

    def own_start(j, i, *targets):
        for c, device in targets:
            own_copy(j, i, c, device).start()
            sent.append(lambda c=c, device=device: own_copy(j, i, c, device))

    def own_wait(j, i, zz, xx, h):
        where = piece(j, zz, xx, half_of(h))
        remote(where, where, ag_send.at[j, i], ag_recv.at[j, i + h], mate).wait_recv()

    def p_of(h):
        return (h * (BLOCK - half), half)

    def q_of(h):
        return (half + h * (q_rows // 2), q_rows // 2)

    def half_of(h):
        return (h * ROWS, ROWS)

    def gather_own_z(j):
        own_start(j, 2, (core, up), (other, up_other))
        own_start(j, 4, (other, down_other), (core, down))

    def gather_own_x(j):
        own_start(j, 0, (core, mate), (other, mate_other))
        w_swap(j).start()

    def gather_1(j):
        own_wait(j, 2, z_down, x, core)
        ag_start(j, 10, z_down, x, half_of(core), up)
        ag_start(j, 12, z_down, x, q_of(core), mate)
        own_wait(j, 4, z_up, x, other)
        ag_start(j, 11, z_up, x, half_of(other), down)
        ag_start(j, 15, z_up, x, q_of(other), mate)
        own_wait(j, 0, z, xm, core)
        ag_start(j, 6, z, xm, p_of(core), up)
        own_wait(j, 0, z, xm, other)
        ag_start(j, 9, z, xm, p_of(other), down)
        ag_start(j, 8, z, xm, p_of(other), up)
        ag_start(j, 7, z, xm, p_of(core), down)
        own_wait(j, 2, z_down, x, other)
        ag_start(j, 13, z_down, x, q_of(other), mate)
        own_wait(j, 4, z_up, x, core)
        ag_start(j, 14, z_up, x, q_of(core), mate)

    def gather_2(j):
        ag_wait(j, 10, z_far, x, half_of(core))
        ag_start(j, 16, z_far, x, q_of(core), mate)
        ag_wait(j, 11, z_far, x, half_of(other))
        ag_start(j, 17, z_far, x, q_of(other), mate)

    def gather_3(j):
        ag_wait(j, 6, z_down, xm, p_of(core))
        ag_start(j, 18, z_down, xm, p_of(core), up)
        ag_wait(j, 9, z_up, xm, p_of(other))
        ag_start(j, 19, z_up, xm, p_of(other), down)

    def gather_4(j):
        w_loads[j].wait()
        w_swap(j).wait_recv()
        ag_wait(j, 7, z_up, xm, p_of(core))
        ag_wait(j, 8, z_down, xm, p_of(other))
        ag_wait(j, 12, z_down, xm, q_of(core))
        ag_wait(j, 13, z_down, xm, q_of(other))
        ag_wait(j, 14, z_up, xm, q_of(core))
        ag_wait(j, 15, z_up, xm, q_of(other))
        ag_wait(j, 16, z_far, xm, q_of(core))
        ag_wait(j, 17, z_far, xm, q_of(other))
        ag_wait(j, 18, z_far, xm, p_of(core))
        ag_wait(j, 19, z_far, xm, p_of(other))

    def tile_copy(c, i):
        where = normed.at[tile_of(c, i)]
        return remote(where, where, n_send.at[i], n_recv.at[i], sibling)

    def norm_tile(i):
        where = tile_of(core, i)
        pltpu.make_async_copy(
            normed.at[where], normed.at[where], local.at[token_base + i]
        ).wait()
        for part in range(2):
            rows = pl.ds(
                pl.multiple_of(core * tokens_here + i * TILE + part * (TILE // 2), 64),
                TILE // 2,
            )
            value = normed[rows, :].astype(F32)
            rms = lax.rsqrt(jnp.mean(value * value, axis=-1, keepdims=True) + EPS)
            normed[rows, :] = (value * rms * gain_v[...]).astype(BF16)
        tile_copy(core, i).start()

    steps = tokens_here // STEP

    def values_step(j, s):
        side = jnp.where(s < steps, core, other)
        inner = lax.rem(s, steps) * STEP
        rows = pl.ds(pl.multiple_of(side * tokens_here + inner, STEP), STEP)
        values = jnp.dot(normed[rows, :], full[j], preferred_element_type=F32) * scale
        goal = tgt[
            side, pl.ds(pl.multiple_of(inner, STEP), STEP), j * CHUNK : (j + 1) * CHUNK
        ].astype(F32)
        err[rows, :] = (values - goal).astype(BF16)

    def grad_step(j, s):
        i = s // 2
        dz = jnp.where(i == 0, 2, jnp.where(i == 1, 1, jnp.where(i == 2, 3, 0)))
        block = lax.rem(z + dz, 4) * 2 + jnp.where(lax.rem(s, 2) == 0, 1 - x, x)
        where = pl.ds(pl.multiple_of(block * BLOCK, 128), BLOCK)
        part = lax.dot_general(
            normed[:, where], err[...], (((0,), (0,)), ((), ())), preferred_element_type=F32
        )
        grad[j, s] = part
        grad_half[j, s] = part.astype(BF16)

    def rs_copy(j, i, src, dst, device):
        return remote(src, dst, rs_send.at[j, i], rs_recv.at[j, i], device)

    def rs_start(j, i, src, dst, device):
        rs_copy(j, i, src, dst, device).start()
        is_total, count = src.dtype == F32, src.shape[0]

        def again():
            where = (total if is_total else grad_half.at[j]).at[0, pl.ds(0, count)]
            return rs_copy(j, i, where, where, mate)

        sent.append(again)

    def rs_wait(j, i, dst):
        rs_copy(j, i, dst, dst, mate).wait_recv()

    def out_of(j, s, part):
        return grad_half.at[j, s, pl.ds(*part)]

    far_p = ((0, half), (half, half))
    far_q = (2 * half, q_rows // 2)
    mate_pa, mate_pb = (BLOCK, half), (BLOCK + half, half)

    def near_at(j, d, part):
        return near.at[j, d, pl.ds(*part)]

    def far_at(j, d, part):
        return far.at[j, d, pl.ds(*part)]

    def scatter_q(j, i):
        rs_start(j, i, out_of(j, 2 * i, Q), from_mate.at[j, i], mate)

    def scatter_far(j):
        for c in range(2):
            rs_start(j, 4 + c, out_of(j, c, PA), far_at(j, 0, far_p[c]), up)
            rs_start(j, 6 + c, out_of(j, c, PB), far_at(j, 1, far_p[c]), down)

    def scatter_up(j):
        rs_start(j, 8, out_of(j, 2, PB), near_at(j, 0, mate_pb), up)
        rs_start(j, 9, out_of(j, 3, PB), near_at(j, 0, PB), up)

    def scatter_down(j):
        rs_start(j, 10, out_of(j, 4, PA), near_at(j, 1, mate_pa), down)
        rs_start(j, 11, out_of(j, 5, PA), near_at(j, 1, PA), down)

    def add_and_send(j, s, part, terms, i, dst, device):
        where = pl.ds(*part)
        value = grad[j, s, where, :]
        for term in terms:
            value = value + term[...].astype(F32)
        grad_half[j, s, where, :] = value.astype(BF16)
        rs_start(j, i, out_of(j, s, part), dst, device)

    def relay_p(j):
        for c in range(2):
            rs_wait(j, 4 + c, far_at(j, 0, far_p[c]))
            dst = near_at(j, 0, PA if c else mate_pa)
            add_and_send(j, 2 + c, PA, [far_at(j, 0, far_p[c])], 12 + c, dst, up)
            rs_wait(j, 6 + c, far_at(j, 1, far_p[c]))
            dst = near_at(j, 1, PB if c else mate_pb)
            add_and_send(j, 4 + c, PB, [far_at(j, 1, far_p[c])], 14 + c, dst, down)

    def mate_q(j, i, lower):
        start, count = (0, q_rows // 2) if lower else (q_rows // 2, q_rows // 2)
        return from_mate.at[j, i, pl.ds(start, count)]

    def far_q_send(j):
        rs_wait(j, 0, from_mate.at[j, 0])
        add_and_send(j, 1, QA, [mate_q(j, 0, True)], 16, far_at(j, 0, far_q), up)
        add_and_send(j, 1, QB, [mate_q(j, 0, False)], 17, far_at(j, 1, far_q), down)

    def near_q_up(j):
        rs_wait(j, 1, from_mate.at[j, 1])
        add_and_send(j, 3, QB, [mate_q(j, 1, False)], 18, near_at(j, 0, QB), up)

    def near_q_down(j):
        rs_wait(j, 2, from_mate.at[j, 2])
        add_and_send(j, 5, QA, [mate_q(j, 2, True)], 19, near_at(j, 1, QA), down)

    def relay_q(j):
        rs_wait(j, 16, far_at(j, 0, far_q))
        terms = [mate_q(j, 1, True), far_at(j, 0, far_q)]
        add_and_send(j, 3, QA, terms, 20, near_at(j, 0, QA), up)
        rs_wait(j, 17, far_at(j, 1, far_q))
        terms = [mate_q(j, 2, False), far_at(j, 1, far_q)]
        add_and_send(j, 5, QB, terms, 21, near_at(j, 1, QB), down)

    def mate_send(j):
        rs_wait(j, 12, near_at(j, 0, mate_pa))
        rs_wait(j, 10, near_at(j, 1, mate_pa))
        terms = [near_at(j, 0, mate_pa), near_at(j, 1, mate_pa)]
        add_and_send(j, 6, PA, terms, 22, mate_p.at[j, 0], mate)
        rs_wait(j, 8, near_at(j, 0, mate_pb))
        rs_wait(j, 14, near_at(j, 1, mate_pb))
        terms = [near_at(j, 0, mate_pb), near_at(j, 1, mate_pb)]
        add_and_send(j, 6, PB, terms, 23, mate_p.at[j, 1], mate)

    def most_of_total(j):
        rs_wait(j, 3, from_mate.at[j, 3])
        for i, d, part in (
            (13, 0, PA),
            (11, 1, PA),
            (9, 0, PB),
            (15, 1, PB),
            (20, 0, QA),
            (19, 1, QA),
            (18, 0, QB),
            (21, 1, QB),
        ):
            rs_wait(j, i, near_at(j, d, part))
        value = grad[j, 7] + near[j, 0, :BLOCK, :].astype(F32)
        total[j] = value + near[j, 1, :BLOCK, :].astype(F32)
        total[j, half : half + q_rows, :] += from_mate[j, 3].astype(F32)

    def rest_of_total(j):
        rs_wait(j, 22, mate_p.at[j, 0])
        rs_wait(j, 23, mate_p.at[j, 1])
        for h in (other, core):
            where = pl.ds(pl.multiple_of(h * (BLOCK - half), 16), half)
            total[j, where, :] += mate_p[j, h].astype(F32)
            if h is other:
                theirs = pl.ds(pl.multiple_of(other * ROWS, 64), ROWS)
                rs_start(j, 24, total.at[j, theirs], swapped.at[j], sibling)

    def update(c, j, gradient):
        columns = cols(c, j)
        fast = own_w[:, columns].astype(F32) - INNER_RATE * (gradient * scale)
        mixed = 0.5 * fast + 0.5 * partner[:, columns].astype(F32)
        base = anchor_v[:, columns]
        moment = SLOW_BETA * momentum_v[:, columns] + (base - mixed) / INNER_RATE
        new_momentum[:, columns] = moment
        new_anchor[:, columns] = base - OUTER_RATE * INNER_RATE * moment

    def update_own(j):
        mine = pl.ds(pl.multiple_of(core * ROWS, 64), ROWS)
        update(core, j, total[j, mine, :])

    def update_other(j):
        rs_wait(j, 24, swapped.at[j])
        update(other, j, swapped[j])

    def drain():
        for copy in sent:
            copy().wait_send()
        sent.clear()

    def when(s, step, *todo):
        @pl.when(s == step)
        def _():
            for do in todo:
                do()

    def friend_part(i):
        if mask == 1:
            friend_swap(i).start()

    gather_own_x(0)
    gather_own_z(0)
    if mask != 1:
        for i in range(FRIEND_PARTS):
            friend_swap(i).start()
    friend_part(0)
    tgt_swap.start()
    gain_load.wait()

    @pl.loop(0, tiles)
    def _(i):
        norm_tile(i)

    gather_1(0)
    gather_2(0)
    gather_own_x(1)
    friend_part(1)
    gather_3(0)
    gather_own_z(1)
    gather_4(0)
    tgt_load.wait()

    @pl.loop(0, steps)
    def _(s):
        values_step(0, s)

    gather_1(1)
    tgt_swap.wait_recv()

    @pl.loop(0, tiles)
    def _(i):
        tile_copy(other, i).wait_recv()

    @pl.loop(steps, 2 * steps)
    def _(s):
        values_step(0, s)

    gather_2(1)

    @pl.loop(0, 8)
    def _(s):
        grad_step(0, s)
        when(s, 1, lambda: scatter_far(0))
        when(
            s,
            3,
            lambda: gather_3(1),
            lambda: scatter_q(0, 0),
            lambda: scatter_up(0),
            lambda: scatter_q(0, 1),
        )
        when(s, 5, lambda: scatter_q(0, 2), lambda: scatter_down(0))
        when(s, 7, lambda: scatter_q(0, 3), lambda: friend_part(2))

    gather_4(1)

    @pl.loop(0, 2 * steps)
    def _(s):
        values_step(1, s)
        when(s, 0, lambda: relay_p(0))
        when(s, 1, lambda: far_q_send(0))
        when(s, 3, lambda: near_q_up(0))

    @pl.loop(0, 8)
    def _(s):
        grad_step(1, s)
        when(s, 1, lambda: scatter_far(1))
        when(s, 2, lambda: mate_send(0), lambda: near_q_down(0))
        when(s, 3, lambda: scatter_up(1), lambda: scatter_q(1, 0), lambda: scatter_q(1, 1))
        when(s, 4, lambda: relay_q(0))
        when(s, 5, lambda: scatter_down(1), lambda: scatter_q(1, 2))
        when(s, 7, lambda: scatter_q(1, 3), lambda: friend_part(3))

    own_w_load.wait()
    anchor_load.wait()
    momentum_load.wait()
    if mask != 1:
        for i in range(FRIEND_PARTS):
            friend_swap(i).wait_recv()
    relay_p(1)
    most_of_total(0)
    rest_of_total(0)
    far_q_send(1)
    near_q_up(1)
    mate_send(1)
    near_q_down(1)
    relay_q(1)
    if mask == 1:
        for i in range(FRIEND_PARTS):
            friend_swap(i).wait_recv()
    update_own(0)
    update_other(0)
    most_of_total(1)

    for j in range(CHUNKS):
        w_swap(j).wait_send()
    tgt_swap.wait_send()
    for i in range(FRIEND_PARTS):
        friend_swap(i).wait_send()

    @pl.loop(0, tiles)
    def _(i):
        tile_copy(core, i).wait_send()

    drain()
    rest_of_total(1)
    update_own(1)
    update_other(1)
    drain()


def run(mask, p_rows, collective_id, tokens, target, gain, weights, previous, anchor, momentum):
    rows, width = tokens.shape
    kv = target.shape[1]
    half, q_rows = p_rows // 2, BLOCK - p_rows
    anywhere = pl.BlockSpec(memory_space=pltpu.HBM)
    vmem, dma = pltpu.VMEM, pltpu.SemaphoreType.DMA
    side = CHUNKS * CHUNK
    return pl.pallas_call(
        functools.partial(kernel, mask, p_rows),
        out_shape=(jax.ShapeDtypeStruct((ROWS, kv), F32),) * 2,
        in_specs=[anywhere] * 7,
        out_specs=(pl.BlockSpec(memory_space=pltpu.VMEM),) * 2,
        scratch_shapes=[
            vmem((2 * rows, width), BF16),
            vmem((CHUNKS, width, CHUNK), BF16),
            vmem((CHUNKS, 8, BLOCK, CHUNK), F32),
            vmem((CHUNKS, 8, BLOCK, CHUNK), BF16),
            vmem((2, rows, side), BF16),
            vmem((2 * rows, CHUNK), BF16),
            vmem((CHUNKS, 4, q_rows, CHUNK), BF16),
            vmem((CHUNKS, 2, p_rows + q_rows // 2, CHUNK), BF16),
            vmem((CHUNKS, 2, BLOCK + p_rows, CHUNK), BF16),
            vmem((CHUNKS, 2, half, CHUNK), BF16),
            vmem((CHUNKS, BLOCK, CHUNK), F32),
            vmem((CHUNKS, ROWS, CHUNK), F32),
            vmem((ROWS, kv), BF16),
            vmem((ROWS, kv), BF16),
            vmem((ROWS, kv), F32),
            vmem((ROWS, kv), F32),
            vmem((1, width), F32),
            dma((CHUNKS, N_AG)),
            dma((CHUNKS, N_AG)),
            dma((CHUNKS, N_RS)),
            dma((CHUNKS, N_RS)),
            dma((rows // TILE,)),
            dma((rows // TILE,)),
            dma((3 + FRIEND_PARTS,)),
            dma((3 + FRIEND_PARTS,)),
            dma((8 + rows // TILE,)),
        ],
        compiler_params=pltpu.CompilerParams(
            collective_id=collective_id,
            has_side_effects=True,
            vmem_limit_bytes=56 << 20,
        ),
    )(tokens, target, gain, weights, previous, anchor, momentum)


def shards(step_bit, tokens, target, norm_gain, weights, previous, anchor, momentum):
    bit_count = lax.axis_size("rep").bit_length() - 1
    chosen_bit = jnp.remainder(step_bit, jnp.int32(bit_count))
    branches = [
        functools.partial(run, 2**bit, 416 if bit == 0 else 352, bit)
        for bit in range(bit_count)
    ]
    moment_new, anchor_new = lax.switch(
        chosen_bit,
        branches,
        tokens[0],
        target[0],
        norm_gain[None],
        weights[0],
        previous[0],
        anchor[0],
        momentum[0],
    )
    return (moment_new[None], anchor_new[None])


def solution(mesh):
    placed = (
        P(),
        P("rep", "fsdp", None),
        P("rep", "fsdp", None),
        P(),
        P("rep", "fsdp", None),
        P("rep", "fsdp", None),
        P("rep", "fsdp", None),
        P("rep", "fsdp", None),
    )
    return jax.shard_map(
        shards,
        mesh=mesh,
        in_specs=placed,
        out_specs=(P("rep", "fsdp", None), P("rep", "fsdp", None)),
        check_vma=False,
    )
```

```python
import functools

import jax
import jax.numpy as jnp
from jax import lax
from jax.experimental import pallas as pl
from jax.experimental.pallas import tpu as pltpu
from jax.sharding import PartitionSpec as P

EPS = 1e-06
INNER_RATE = 0.05
OUTER_RATE = 1.0
SLOW_BETA = 0.6

MESH = pl.DeviceIdType.MESH
BF16 = jnp.bfloat16
F32 = jnp.float32

ROWS = 320
BLOCK = 2 * ROWS
CHUNK = 256
CHUNKS = 2
FRIEND_PARTS = 4
SPLIT = (352, 352)
SPLIT_X = (416, 416)
TILE = 128
STEP = 512
N_AG = 20
N_RS = 26


def kernel(
    mask,
    p_gather,
    p_rows,
    tokens,
    target,
    gain,
    weights,
    previous,
    anchor,
    momentum,
    new_momentum,
    new_anchor,
    normed,
    full,
    grad,
    grad_half,
    tgt,
    err,
    from_mate,
    far,
    near,
    last,
    last_mate,
    total,
    sibling_own,
    own_w,
    partner,
    anchor_v,
    momentum_v,
    gain_v,
    ag_send,
    ag_recv,
    rs_send,
    rs_recv,
    last_recv,
    n_send,
    n_recv,
    m_send,
    m_recv,
    local,
):
    rep = lax.axis_index("rep")
    at = lax.axis_index("fsdp")
    core = lax.rem(at, 2)
    other = 1 - core
    x = lax.rem(at // 2, 2)
    z = at // 4
    z_up, z_down, z_far = lax.rem(z + 1, 4), lax.rem(z + 3, 4), lax.rem(z + 2, 4)
    up, up_other = [(rep, z_up * 4 + x * 2 + c) for c in (core, other)]
    down, down_other = [(rep, z_down * 4 + x * 2 + c) for c in (core, other)]
    mate, mate_other = [(rep, z * 4 + (1 - x) * 2 + c) for c in (core, other)]
    up_core = [(rep, z_up * 4 + x * 2 + c) for c in range(2)]
    down_core = [(rep, z_down * 4 + x * 2 + c) for c in range(2)]
    mate_core = [(rep, z * 4 + (1 - x) * 2 + c) for c in range(2)]
    sibling = (rep, z * 4 + x * 2 + other)
    friend = (rep + mask - 2 * mask * lax.rem(rep // mask, 2), at)

    tokens_here, width = tokens.shape
    scale = width ** (-0.5)
    half = p_rows // 2
    q_rows = BLOCK - p_rows
    PA, PB = (0, half), (BLOCK - half, half)
    QA, QB, Q = (half, q_rows // 2), (ROWS, q_rows // 2), (half, q_rows)

    def remote(src, dst, send, recv, device):
        return pltpu.make_async_remote_copy(
            src_ref=src,
            dst_ref=dst,
            send_sem=send,
            recv_sem=recv,
            device_id=device,
            device_id_type=MESH,
        )

    sent = []

    barrier = pltpu.get_barrier_semaphore()
    everyone = (up, up_other, down, down_other, mate, mate_other, sibling, friend)
    for device in everyone:
        pl.semaphore_signal(barrier, inc=1, device_id=device, device_id_type=MESH)

    def load(src, dst, i):
        copy = pltpu.make_async_copy(src, dst, local.at[i])
        copy.start()
        return copy

    def cols(c, j):
        return pl.ds(pl.multiple_of(c * CHUNKS * CHUNK + j * CHUNK, CHUNK), CHUNK)

    def half_cols(c):
        return pl.ds(pl.multiple_of(c * CHUNKS * CHUNK, CHUNK), CHUNKS * CHUNK)

    own_base = (z * 2 + x) * BLOCK

    def own_rows(c):
        return pl.ds(pl.multiple_of(own_base + c * ROWS, 64), ROWS)

    w_loads = [
        load(weights.at[:, cols(core, j)], full.at[j, own_rows(core)], j)
        for j in range(CHUNKS)
    ]
    tiles = tokens_here // TILE

    def tile_of(c, i):
        return pl.ds(pl.multiple_of(c * tokens_here + i * TILE, TILE), TILE)

    gain_load = load(gain, gain_v, 2)
    token_base = 8

    @pl.loop(0, tiles)
    def _(i):
        rows = pl.ds(pl.multiple_of(i * TILE, TILE), TILE)
        pltpu.make_async_copy(
            tokens.at[rows], normed.at[tile_of(core, i)], local.at[token_base + i]
        ).start()

    tgt_load = load(target.at[:, half_cols(core)], tgt.at[core], 3)
    own_w_load = load(weights, own_w, 4)
    anchor_load = load(anchor, anchor_v, 5)
    momentum_load = load(momentum, momentum_v, 6)

    pl.semaphore_wait(barrier, len(everyone))

    def w_swap(j):
        return remote(
            weights.at[:, cols(other, j)],
            full.at[j, own_rows(core)],
            m_send.at[j],
            m_recv.at[j],
            sibling,
        )
    tgt_swap = remote(
        target.at[:, half_cols(other)], tgt.at[core], m_send.at[2], m_recv.at[2], sibling
    )
    friend_rows = ROWS // FRIEND_PARTS

    def friend_swap(i):
        where = pl.ds(i * friend_rows, friend_rows)
        return remote(
            previous.at[where], partner.at[where], m_send.at[3 + i], m_recv.at[3 + i], friend
        )

    def piece(j, zz, xx, part):
        start = pl.multiple_of((zz * 2 + xx) * BLOCK + part[0], 16)
        return full.at[j, pl.ds(start, part[1])]

    def ag_copy(j, i, zz, xx, part, device):
        where = piece(j, zz, xx, part)
        return remote(where, where, ag_send.at[j, i], ag_recv.at[j, i], device)

    def ag_start(j, i, zz, xx, part, device):
        ag_copy(j, i, zz, xx, part, device).start()
        sent.append(lambda: ag_copy(j, i, z, x, (0, part[1]), mate))

    def ag_wait(j, i, zz, xx, part):
        ag_copy(j, i, zz, xx, part, mate).wait_recv()

    xm = 1 - x

    def own_copy(j, i, c, device):
        return remote(
            weights.at[:, cols(c, j)],
            full.at[j, own_rows(core)],
            ag_send.at[j, i + jnp.where(c == core, 0, 1)],
            ag_recv.at[j, i + core],
            device,
        )

    def own_start(j, i, *targets):
        for c, device in targets:
            own_copy(j, i, c, device).start()
            sent.append(lambda c=c, device=device: own_copy(j, i, c, device))

    def own_wait(j, i, zz, xx, h):
        where = piece(j, zz, xx, half_of(h))
        remote(where, where, ag_send.at[j, i], ag_recv.at[j, i + h], mate).wait_recv()

    p_half = p_gather // 2
    q_half = ROWS - p_half

    def p_of(h):
        return (h * (BLOCK - p_half), p_half)

    def q_of(h):
        return (p_half + h * q_half, q_half)

    def half_of(h):
        return (h * ROWS, ROWS)

    def gather_own_z(j):
        own_start(j, 2, (core, up), (other, up_other))
        own_start(j, 4, (other, down_other), (core, down))

    def gather_own_x(j):
        own_start(j, 0, (core, mate), (other, mate_other))
        w_swap(j).start()

    def gather_1(j):
        own_wait(j, 2, z_down, x, core)
        ag_start(j, 10, z_down, x, half_of(core), up)
        ag_start(j, 12, z_down, x, q_of(core), mate)
        own_wait(j, 4, z_up, x, other)
        ag_start(j, 11, z_up, x, half_of(other), down)
        ag_start(j, 15, z_up, x, q_of(other), mate)
        own_wait(j, 0, z, xm, core)
        ag_start(j, 6, z, xm, p_of(core), up)

    def gather_1_rest(j):
        own_wait(j, 0, z, xm, other)
        ag_start(j, 9, z, xm, p_of(other), down)
        ag_start(j, 8, z, xm, p_of(other), up)
        ag_start(j, 7, z, xm, p_of(core), down)
        own_wait(j, 2, z_down, x, other)
        ag_start(j, 13, z_down, x, q_of(other), mate)
        own_wait(j, 4, z_up, x, core)
        ag_start(j, 14, z_up, x, q_of(core), mate)

    def gather_2(j):
        ag_wait(j, 10, z_far, x, half_of(core))
        ag_start(j, 16, z_far, x, q_of(core), mate)
        ag_wait(j, 11, z_far, x, half_of(other))
        ag_start(j, 17, z_far, x, q_of(other), mate)

    def gather_3(j):
        ag_wait(j, 6, z_down, xm, p_of(core))
        ag_start(j, 18, z_down, xm, p_of(core), up)
        ag_wait(j, 9, z_up, xm, p_of(other))
        ag_start(j, 19, z_up, xm, p_of(other), down)

    def gather_4(j):
        w_loads[j].wait()
        w_swap(j).wait_recv()
        ag_wait(j, 7, z_up, xm, p_of(core))
        ag_wait(j, 8, z_down, xm, p_of(other))
        ag_wait(j, 12, z_down, xm, q_of(core))
        ag_wait(j, 13, z_down, xm, q_of(other))
        ag_wait(j, 14, z_up, xm, q_of(core))
        ag_wait(j, 15, z_up, xm, q_of(other))
        ag_wait(j, 16, z_far, xm, q_of(core))
        ag_wait(j, 17, z_far, xm, q_of(other))
        ag_wait(j, 18, z_far, xm, p_of(core))
        ag_wait(j, 19, z_far, xm, p_of(other))

    def tile_copy(c, i):
        where = normed.at[tile_of(c, i)]
        return remote(where, where, n_send.at[i], n_recv.at[i], sibling)

    def norm_tile(i):
        where = tile_of(core, i)
        pltpu.make_async_copy(
            normed.at[where], normed.at[where], local.at[token_base + i]
        ).wait()
        for part in range(2):
            rows = pl.ds(
                pl.multiple_of(core * tokens_here + i * TILE + part * (TILE // 2), 64),
                TILE // 2,
            )
            value = normed[rows, :].astype(F32)
            rms = lax.rsqrt(jnp.mean(value * value, axis=-1, keepdims=True) + EPS)
            normed[rows, :] = (value * rms * gain_v[...]).astype(BF16)
        tile_copy(core, i).start()

    steps = tokens_here // STEP

    def values_step(j, s):
        side = jnp.where(s < steps, core, other)
        inner = lax.rem(s, steps) * STEP
        rows = pl.ds(pl.multiple_of(side * tokens_here + inner, STEP), STEP)
        values = jnp.dot(normed[rows, :], full[j], preferred_element_type=F32) * scale
        goal = tgt[
            side, pl.ds(pl.multiple_of(inner, STEP), STEP), j * CHUNK : (j + 1) * CHUNK
        ].astype(F32)
        err[rows, :] = (values - goal).astype(BF16)

    def grad_step(j, s):
        i = s // 2
        dz = jnp.where(i == 0, 2, jnp.where(i == 1, 1, jnp.where(i == 2, 3, 0)))
        block = lax.rem(z + dz, 4) * 2 + jnp.where(lax.rem(s, 2) == 0, 1 - x, x)
        where = pl.ds(pl.multiple_of(block * BLOCK, 128), BLOCK)
        part = lax.dot_general(
            normed[:, where], err[...], (((0,), (0,)), ((), ())), preferred_element_type=F32
        )
        grad[j, s] = part
        grad_half[j, s] = part.astype(BF16)

    def rs_copy(j, i, src, dst, device):
        return remote(src, dst, rs_send.at[j, i], rs_recv.at[j, i], device)

    def rs_sent(j, i, src):
        whole, count = src.dtype == F32, src.shape[0]

        def again():
            where = sibling_own.at[j] if whole else grad_half.at[j, 0, pl.ds(0, count)]
            return rs_copy(j, i, where, where, mate)

        sent.append(again)

    def rs_start(j, i, src, dst, device):
        rs_copy(j, i, src, dst, device).start()
        rs_sent(j, i, src)

    P_LAST, Q_LAST = pl.ds(0, half), pl.ds(half, q_rows // 2)

    def last_at(j, c, kind):
        rows = Q_LAST if kind % 2 else P_LAST
        return last_mate.at[j, c, rows] if kind > 3 else last.at[j, c, kind // 2, rows]

    def last_start(j, i, src, kind, h):
        device = (up_core, down_core, mate_core)[kind // 2][h]
        copy = remote(
            src, last_at(j, core, kind), rs_send.at[j, i], last_recv.at[j, core, kind], device
        )
        copy.start()
        rs_sent(j, i, src)

    def last_wait(j, c, kind):
        where = last_at(j, c, kind)
        remote(where, where, rs_send.at[j, 0], last_recv.at[j, c, kind], mate).wait_recv()

    def rs_wait(j, i, dst):
        rs_copy(j, i, dst, dst, mate).wait_recv()

    def out_of(j, s, part):
        return grad_half.at[j, s, pl.ds(*part)]

    far_p = ((0, half), (half, half))
    far_q = (2 * half, q_rows // 2)
    mate_pa, mate_pb = (0, half), (half, half)

    def near_at(j, d, part):
        return near.at[j, d, pl.ds(*part)]

    def far_at(j, d, part):
        return far.at[j, d, pl.ds(*part)]

    def scatter_q(j, i):
        if i < 3:
            rs_start(j, i, out_of(j, 2 * i, Q), from_mate.at[j, i], mate)
        else:
            last_start(j, 3, out_of(j, 6, QA), 5, 0)
            last_start(j, 25, out_of(j, 6, QB), 5, 1)

    def scatter_far(j):
        for c in range(2):
            rs_start(j, 4 + c, out_of(j, c, PA), far_at(j, 0, far_p[c]), up)
            rs_start(j, 6 + c, out_of(j, c, PB), far_at(j, 1, far_p[c]), down)

    def scatter_up(j):
        rs_start(j, 8, out_of(j, 2, PB), near_at(j, 0, mate_pb), up)
        last_start(j, 9, out_of(j, 3, PB), 0, 1)

    def scatter_down(j):
        rs_start(j, 10, out_of(j, 4, PA), near_at(j, 1, mate_pa), down)
        last_start(j, 11, out_of(j, 5, PA), 2, 0)

    def scatter_own(j):
        theirs = pl.ds(pl.multiple_of(other * ROWS, 64), ROWS)
        rs_start(j, 24, grad.at[j, 7, theirs], sibling_own.at[j], sibling)

    def added(j, s, part, terms):
        where = pl.ds(*part)
        value = grad[j, s, where, :]
        for term in terms:
            value = value + term[...].astype(F32)
        grad_half[j, s, where, :] = value.astype(BF16)
        return out_of(j, s, part)

    def relay_p(j):
        rs_wait(j, 4, far_at(j, 0, far_p[0]))
        rs_start(j, 12, added(j, 2, PA, [far_at(j, 0, far_p[0])]), near_at(j, 0, mate_pa), up)
        rs_wait(j, 6, far_at(j, 1, far_p[0]))
        rs_start(j, 14, added(j, 4, PB, [far_at(j, 1, far_p[0])]), near_at(j, 1, mate_pb), down)
        rs_wait(j, 5, far_at(j, 0, far_p[1]))
        last_start(j, 13, added(j, 3, PA, [far_at(j, 0, far_p[1])]), 0, 0)
        rs_wait(j, 7, far_at(j, 1, far_p[1]))
        last_start(j, 15, added(j, 5, PB, [far_at(j, 1, far_p[1])]), 2, 1)

    def mate_q(j, i, lower):
        start, count = (0, q_rows // 2) if lower else (q_rows // 2, q_rows // 2)
        return from_mate.at[j, i, pl.ds(start, count)]

    def far_q_send(j):
        rs_wait(j, 0, from_mate.at[j, 0])
        rs_start(j, 16, added(j, 1, QA, [mate_q(j, 0, True)]), far_at(j, 0, far_q), up)
        rs_start(j, 17, added(j, 1, QB, [mate_q(j, 0, False)]), far_at(j, 1, far_q), down)

    def near_q_up(j):
        rs_wait(j, 1, from_mate.at[j, 1])
        last_start(j, 18, added(j, 3, QB, [mate_q(j, 1, False)]), 1, 1)

    def near_q_down(j):
        rs_wait(j, 2, from_mate.at[j, 2])
        last_start(j, 19, added(j, 5, QA, [mate_q(j, 2, True)]), 3, 0)

    def relay_q(j):
        rs_wait(j, 16, far_at(j, 0, far_q))
        terms = [mate_q(j, 1, True), far_at(j, 0, far_q)]
        last_start(j, 20, added(j, 3, QA, terms), 1, 0)
        rs_wait(j, 17, far_at(j, 1, far_q))
        terms = [mate_q(j, 2, False), far_at(j, 1, far_q)]
        last_start(j, 21, added(j, 5, QB, terms), 3, 1)

    def mate_send(j):
        rs_wait(j, 12, near_at(j, 0, mate_pa))
        rs_wait(j, 10, near_at(j, 1, mate_pa))
        terms = [near_at(j, 0, mate_pa), near_at(j, 1, mate_pa)]
        last_start(j, 22, added(j, 6, PA, terms), 4, 0)
        rs_wait(j, 8, near_at(j, 0, mate_pb))
        rs_wait(j, 14, near_at(j, 1, mate_pb))
        terms = [near_at(j, 0, mate_pb), near_at(j, 1, mate_pb)]
        last_start(j, 23, added(j, 6, PB, terms), 4, 1)

    p_start, q_start = core * (q_rows // 2), other * half

    def most_of_total(j):
        rs_wait(j, 24, sibling_own.at[j])
        for k, c in enumerate((core, other)):
            for kind in (0, 2, 1, 3, 5):
                last_wait(j, c, kind)
            for start, rows, part in ((p_start, P_LAST, half), (q_start, Q_LAST, q_rows // 2)):
                here = pl.ds(pl.multiple_of(start, 16), part)
                if k:
                    value = sibling_own[j, here, :]
                else:
                    value = grad[j, 7, pl.ds(pl.multiple_of(core * ROWS + start, 16), part), :]
                value = value + last[j, c, 0, rows, :].astype(F32)
                value = value + last[j, c, 1, rows, :].astype(F32)
                if rows is Q_LAST:
                    value = value + last_mate[j, c, rows, :].astype(F32)
                total[j, k, here, :] = value

    def rest_of_total(j):
        for k, c in enumerate((core, other)):
            last_wait(j, c, 4)
            here = pl.ds(pl.multiple_of(p_start, 16), half)
            total[j, k, here, :] += last_mate[j, c, P_LAST, :].astype(F32)
            update(c, j, total[j, k])

    def update(c, j, gradient):
        columns = cols(c, j)
        fast = own_w[:, columns].astype(F32) - INNER_RATE * (gradient * scale)
        mixed = 0.5 * fast + 0.5 * partner[:, columns].astype(F32)
        base = anchor_v[:, columns]
        moment = SLOW_BETA * momentum_v[:, columns] + (base - mixed) / INNER_RATE
        new_momentum[:, columns] = moment
        new_anchor[:, columns] = base - OUTER_RATE * INNER_RATE * moment

    def drain():
        for copy in sent:
            copy().wait_send()
        sent.clear()

    def when(s, step, *todo):
        @pl.when(s == step)
        def _():
            for do in todo:
                do()

    def friend_part(i):
        if mask == 1:
            friend_swap(i).start()

    gather_own_x(0)
    gather_own_z(0)
    if mask != 1:
        for i in range(FRIEND_PARTS):
            friend_swap(i).start()
    friend_part(0)
    tgt_swap.start()
    gain_load.wait()

    @pl.loop(0, tiles)
    def _(i):
        norm_tile(i)

    gather_1(0)
    gather_1_rest(0)
    gather_2(0)
    gather_own_x(1)
    friend_part(1)
    gather_3(0)
    gather_own_z(1)
    gather_4(0)
    tgt_load.wait()

    @pl.loop(0, steps)
    def _(s):
        values_step(0, s)
        when(s, 0, lambda: gather_1(1))

    tgt_swap.wait_recv()

    @pl.loop(0, tiles)
    def _(i):
        tile_copy(other, i).wait_recv()

    @pl.loop(steps, 2 * steps)
    def _(s):
        values_step(0, s)
        when(s, steps, lambda: gather_1_rest(1))

    @pl.loop(0, 8)
    def _(s):
        grad_step(0, s)
        when(s, 1, lambda: gather_2(1), lambda: scatter_far(0))
        when(
            s,
            3,
            lambda: gather_3(1),
            lambda: scatter_q(0, 0),
            lambda: scatter_up(0),
            lambda: scatter_q(0, 1),
        )
        when(s, 5, lambda: scatter_q(0, 2), lambda: scatter_down(0))
        when(s, 7, lambda: scatter_own(0), lambda: scatter_q(0, 3), lambda: friend_part(2))

    gather_4(1)

    @pl.loop(0, 2 * steps)
    def _(s):
        values_step(1, s)
        when(s, 0, lambda: relay_p(0))
        when(s, 1, lambda: far_q_send(0))
        when(s, 3, lambda: near_q_up(0))

    @pl.loop(0, 8)
    def _(s):
        grad_step(1, s)
        when(s, 0, lambda: near_q_down(0))
        when(s, 1, lambda: scatter_far(1), lambda: scatter_q(1, 0))
        when(s, 2, lambda: mate_send(0))
        when(s, 3, lambda: scatter_up(1), lambda: scatter_q(1, 1), lambda: relay_q(0))
        when(s, 5, lambda: scatter_down(1), lambda: scatter_q(1, 2))
        when(s, 7, lambda: scatter_own(1), lambda: scatter_q(1, 3), lambda: friend_part(3))

    own_w_load.wait()
    anchor_load.wait()
    momentum_load.wait()
    if mask != 1:
        for i in range(FRIEND_PARTS):
            friend_swap(i).wait_recv()
    relay_p(1)
    most_of_total(0)
    far_q_send(1)
    near_q_up(1)
    mate_send(1)
    near_q_down(1)
    relay_q(1)
    if mask == 1:
        for i in range(FRIEND_PARTS):
            friend_swap(i).wait_recv()
    rest_of_total(0)
    most_of_total(1)

    for j in range(CHUNKS):
        w_swap(j).wait_send()
    tgt_swap.wait_send()
    for i in range(FRIEND_PARTS):
        friend_swap(i).wait_send()

    @pl.loop(0, tiles)
    def _(i):
        tile_copy(core, i).wait_send()

    drain()
    rest_of_total(1)


def run(mask, p_gather, p_rows, collective_id, tokens, target, gain, weights, previous, anchor, momentum):
    rows, width = tokens.shape
    kv = target.shape[1]
    half, q_rows = p_rows // 2, BLOCK - p_rows
    anywhere = pl.BlockSpec(memory_space=pltpu.HBM)
    vmem, dma = pltpu.VMEM, pltpu.SemaphoreType.DMA
    side = CHUNKS * CHUNK
    return pl.pallas_call(
        functools.partial(kernel, mask, p_gather, p_rows),
        out_shape=(jax.ShapeDtypeStruct((ROWS, kv), F32),) * 2,
        in_specs=[anywhere] * 7,
        out_specs=(pl.BlockSpec(memory_space=pltpu.VMEM),) * 2,
        scratch_shapes=[
            vmem((2 * rows, width), BF16),
            vmem((CHUNKS, width, CHUNK), BF16),
            vmem((CHUNKS, 8, BLOCK, CHUNK), F32),
            vmem((CHUNKS, 8, BLOCK, CHUNK), BF16),
            vmem((2, rows, side), BF16),
            vmem((2 * rows, CHUNK), BF16),
            vmem((CHUNKS, 3, q_rows, CHUNK), BF16),
            vmem((CHUNKS, 2, p_rows + q_rows // 2, CHUNK), BF16),
            vmem((CHUNKS, 2, p_rows, CHUNK), BF16),
            vmem((CHUNKS, 2, 2, ROWS, CHUNK), BF16),
            vmem((CHUNKS, 2, ROWS, CHUNK), BF16),
            vmem((CHUNKS, 2, ROWS, CHUNK), F32),
            vmem((CHUNKS, ROWS, CHUNK), F32),
            vmem((ROWS, kv), BF16),
            vmem((ROWS, kv), BF16),
            vmem((ROWS, kv), F32),
            vmem((ROWS, kv), F32),
            vmem((1, width), F32),
            dma((CHUNKS, N_AG)),
            dma((CHUNKS, N_AG)),
            dma((CHUNKS, N_RS)),
            dma((CHUNKS, N_RS)),
            dma((CHUNKS, 2, 6)),
            dma((rows // TILE,)),
            dma((rows // TILE,)),
            dma((3 + FRIEND_PARTS,)),
            dma((3 + FRIEND_PARTS,)),
            dma((8 + rows // TILE,)),
        ],
        compiler_params=pltpu.CompilerParams(
            collective_id=collective_id,
            has_side_effects=True,
            vmem_limit_bytes=56 << 20,
        ),
    )(tokens, target, gain, weights, previous, anchor, momentum)


def shards(step_bit, tokens, target, norm_gain, weights, previous, anchor, momentum):
    bit_count = lax.axis_size("rep").bit_length() - 1
    chosen_bit = jnp.remainder(step_bit, jnp.int32(bit_count))
    branches = [
        functools.partial(run, 2**bit, *(SPLIT_X if bit == 0 else SPLIT), bit)
        for bit in range(bit_count)
    ]
    moment_new, anchor_new = lax.switch(
        chosen_bit,
        branches,
        tokens[0],
        target[0],
        norm_gain[None],
        weights[0],
        previous[0],
        anchor[0],
        momentum[0],
    )
    return (moment_new[None], anchor_new[None])


def solution(mesh):
    placed = (
        P(),
        P("rep", "fsdp", None),
        P("rep", "fsdp", None),
        P(),
        P("rep", "fsdp", None),
        P("rep", "fsdp", None),
        P("rep", "fsdp", None),
        P("rep", "fsdp", None),
    )
    return jax.shard_map(
        shards,
        mesh=mesh,
        in_specs=placed,
        out_specs=(P("rep", "fsdp", None), P("rep", "fsdp", None)),
        check_vma=False,
    )
```

```python
import functools

import jax
import jax.numpy as jnp
from jax import lax
from jax.experimental import pallas as pl
from jax.experimental.pallas import tpu as pltpu
from jax.sharding import PartitionSpec as P

EPS = 1e-06
INNER_RATE = 0.05
OUTER_RATE = 1.0
SLOW_BETA = 0.6

MESH = pl.DeviceIdType.MESH
BF16 = jnp.bfloat16
F32 = jnp.float32

ROWS = 320
BLOCK = 2 * ROWS
CHUNK = 256
CHUNKS = 2
FRIEND_PARTS = 4
SPLIT = (352, 352)
SPLIT_X = (416, 416)
TILE = 128
STEP = 512
N_AG = 20
N_RS = 26


def kernel(
    mask,
    p_gather,
    p_rows,
    tokens,
    target,
    gain,
    weights,
    previous,
    anchor,
    momentum,
    new_momentum,
    new_anchor,
    normed,
    full,
    grad,
    grad_half,
    tgt,
    err,
    from_mate,
    far,
    near,
    last,
    last_mate,
    total,
    sibling_own,
    own_w,
    partner,
    anchor_v,
    momentum_v,
    gain_v,
    ag_send,
    ag_recv,
    rs_send,
    rs_recv,
    last_recv,
    n_send,
    n_recv,
    m_send,
    m_recv,
    local,
):
    rep = lax.axis_index("rep")
    at = lax.axis_index("fsdp")
    core = lax.rem(at, 2)
    other = 1 - core
    x = lax.rem(at // 2, 2)
    z = at // 4
    z_up, z_down, z_far = lax.rem(z + 1, 4), lax.rem(z + 3, 4), lax.rem(z + 2, 4)
    up, up_other = [(rep, z_up * 4 + x * 2 + c) for c in (core, other)]
    down, down_other = [(rep, z_down * 4 + x * 2 + c) for c in (core, other)]
    mate, mate_other = [(rep, z * 4 + (1 - x) * 2 + c) for c in (core, other)]
    up_core = [(rep, z_up * 4 + x * 2 + c) for c in range(2)]
    down_core = [(rep, z_down * 4 + x * 2 + c) for c in range(2)]
    mate_core = [(rep, z * 4 + (1 - x) * 2 + c) for c in range(2)]
    sibling = (rep, z * 4 + x * 2 + other)
    friend = (rep + mask - 2 * mask * lax.rem(rep // mask, 2), at)

    tokens_here, width = tokens.shape
    scale = width ** (-0.5)
    half = p_rows // 2
    q_rows = BLOCK - p_rows
    PA, PB = (0, half), (BLOCK - half, half)
    QA, QB, Q = (half, q_rows // 2), (ROWS, q_rows // 2), (half, q_rows)

    def remote(src, dst, send, recv, device):
        return pltpu.make_async_remote_copy(
            src_ref=src,
            dst_ref=dst,
            send_sem=send,
            recv_sem=recv,
            device_id=device,
            device_id_type=MESH,
        )

    sent = []

    barrier = pltpu.get_barrier_semaphore()
    everyone = (up, up_other, down, down_other, mate, mate_other, sibling, friend)
    for device in everyone:
        pl.semaphore_signal(barrier, inc=1, device_id=device, device_id_type=MESH)

    def load(src, dst, i):
        copy = pltpu.make_async_copy(src, dst, local.at[i])
        copy.start()
        return copy

    def cols(c, j):
        return pl.ds(pl.multiple_of(c * CHUNKS * CHUNK + j * CHUNK, CHUNK), CHUNK)

    def half_cols(c):
        return pl.ds(pl.multiple_of(c * CHUNKS * CHUNK, CHUNK), CHUNKS * CHUNK)

    own_base = (z * 2 + x) * BLOCK

    def own_rows(c):
        return pl.ds(pl.multiple_of(own_base + c * ROWS, 64), ROWS)

    w_loads = [
        load(weights.at[:, cols(core, j)], full.at[j, own_rows(core)], j)
        for j in range(CHUNKS)
    ]
    tiles = tokens_here // TILE

    def tile_of(c, i):
        return pl.ds(pl.multiple_of(c * tokens_here + i * TILE, TILE), TILE)

    gain_load = load(gain, gain_v, 2)
    token_base = 8

    @pl.loop(0, tiles)
    def _(i):
        rows = pl.ds(pl.multiple_of(i * TILE, TILE), TILE)
        pltpu.make_async_copy(
            tokens.at[rows], normed.at[tile_of(core, i)], local.at[token_base + i]
        ).start()

    tgt_load = load(target.at[:, half_cols(core)], tgt.at[core], 3)
    own_w_load = load(weights, own_w, 4)
    anchor_load = load(anchor, anchor_v, 5)
    momentum_load = load(momentum, momentum_v, 6)

    pl.semaphore_wait(barrier, len(everyone))

    def w_swap(j):
        return remote(
            weights.at[:, cols(other, j)],
            full.at[j, own_rows(core)],
            m_send.at[j],
            m_recv.at[j],
            sibling,
        )
    tgt_swap = remote(
        target.at[:, half_cols(other)], tgt.at[core], m_send.at[2], m_recv.at[2], sibling
    )
    friend_rows = ROWS // FRIEND_PARTS

    def friend_swap(i):
        where = pl.ds(i * friend_rows, friend_rows)
        return remote(
            previous.at[where], partner.at[where], m_send.at[3 + i], m_recv.at[3 + i], friend
        )

    def piece(j, zz, xx, part):
        start = pl.multiple_of((zz * 2 + xx) * BLOCK + part[0], 16)
        return full.at[j, pl.ds(start, part[1])]

    def ag_copy(j, i, zz, xx, part, device):
        where = piece(j, zz, xx, part)
        return remote(where, where, ag_send.at[j, i], ag_recv.at[j, i], device)

    def ag_start(j, i, zz, xx, part, device):
        ag_copy(j, i, zz, xx, part, device).start()
        sent.append(lambda: ag_copy(j, i, z, x, (0, part[1]), mate))

    def ag_wait(j, i, zz, xx, part):
        ag_copy(j, i, zz, xx, part, mate).wait_recv()

    xm = 1 - x

    def own_copy(j, i, c, device):
        return remote(
            weights.at[:, cols(c, j)],
            full.at[j, own_rows(core)],
            ag_send.at[j, i + jnp.where(c == core, 0, 1)],
            ag_recv.at[j, i + core],
            device,
        )

    def own_start(j, i, *targets):
        for c, device in targets:
            own_copy(j, i, c, device).start()
            sent.append(lambda c=c, device=device: own_copy(j, i, c, device))

    def own_wait(j, i, zz, xx, h):
        where = piece(j, zz, xx, half_of(h))
        remote(where, where, ag_send.at[j, i], ag_recv.at[j, i + h], mate).wait_recv()

    p_half = p_gather // 2
    q_half = ROWS - p_half

    def p_of(h):
        return (h * (BLOCK - p_half), p_half)

    def q_of(h):
        return (p_half + h * q_half, q_half)

    def half_of(h):
        return (h * ROWS, ROWS)

    def gather_own_z(j):
        own_start(j, 2, (core, up), (other, up_other))
        own_start(j, 4, (other, down_other), (core, down))

    def gather_own_x(j):
        own_start(j, 0, (core, mate), (other, mate_other))
        w_swap(j).start()

    def gather_1(j):
        own_wait(j, 2, z_down, x, core)
        ag_start(j, 10, z_down, x, half_of(core), up)
        ag_start(j, 12, z_down, x, q_of(core), mate)
        own_wait(j, 4, z_up, x, other)
        ag_start(j, 11, z_up, x, half_of(other), down)
        ag_start(j, 15, z_up, x, q_of(other), mate)
        own_wait(j, 0, z, xm, core)
        ag_start(j, 6, z, xm, p_of(core), up)

    def gather_1_rest(j):
        own_wait(j, 0, z, xm, other)
        ag_start(j, 9, z, xm, p_of(other), down)
        ag_start(j, 8, z, xm, p_of(other), up)
        ag_start(j, 7, z, xm, p_of(core), down)
        own_wait(j, 2, z_down, x, other)
        ag_start(j, 13, z_down, x, q_of(other), mate)
        own_wait(j, 4, z_up, x, core)
        ag_start(j, 14, z_up, x, q_of(core), mate)

    def gather_2(j):
        ag_wait(j, 10, z_far, x, half_of(core))
        ag_start(j, 16, z_far, x, q_of(core), mate)
        ag_wait(j, 11, z_far, x, half_of(other))
        ag_start(j, 17, z_far, x, q_of(other), mate)

    def gather_3(j):
        ag_wait(j, 6, z_down, xm, p_of(core))
        ag_start(j, 18, z_down, xm, p_of(core), up)
        ag_wait(j, 9, z_up, xm, p_of(other))
        ag_start(j, 19, z_up, xm, p_of(other), down)

    def gather_4(j):
        w_loads[j].wait()
        w_swap(j).wait_recv()
        ag_wait(j, 7, z_up, xm, p_of(core))
        ag_wait(j, 8, z_down, xm, p_of(other))
        ag_wait(j, 12, z_down, xm, q_of(core))
        ag_wait(j, 13, z_down, xm, q_of(other))
        ag_wait(j, 14, z_up, xm, q_of(core))
        ag_wait(j, 15, z_up, xm, q_of(other))
        ag_wait(j, 16, z_far, xm, q_of(core))
        ag_wait(j, 17, z_far, xm, q_of(other))
        ag_wait(j, 18, z_far, xm, p_of(core))
        ag_wait(j, 19, z_far, xm, p_of(other))

    def tile_copy(c, i):
        where = normed.at[tile_of(c, i)]
        return remote(where, where, n_send.at[i], n_recv.at[i], sibling)

    def norm_tile(i):
        where = tile_of(core, i)
        pltpu.make_async_copy(
            normed.at[where], normed.at[where], local.at[token_base + i]
        ).wait()
        for part in range(2):
            rows = pl.ds(
                pl.multiple_of(core * tokens_here + i * TILE + part * (TILE // 2), 64),
                TILE // 2,
            )
            value = normed[rows, :].astype(F32)
            rms = lax.rsqrt(jnp.mean(value * value, axis=-1, keepdims=True) + EPS)
            normed[rows, :] = (value * rms * gain_v[...]).astype(BF16)
        tile_copy(core, i).start()

    steps = tokens_here // STEP

    def values_step(j, s):
        side = jnp.where(s < steps, core, other)
        inner = lax.rem(s, steps) * STEP
        rows = pl.ds(pl.multiple_of(side * tokens_here + inner, STEP), STEP)
        values = jnp.dot(normed[rows, :], full[j], preferred_element_type=F32) * scale
        goal = tgt[
            side, pl.ds(pl.multiple_of(inner, STEP), STEP), j * CHUNK : (j + 1) * CHUNK
        ].astype(F32)
        err[rows, :] = (values - goal).astype(BF16)

    def grad_step(j, s):
        i = s // 2
        dz = jnp.where(i == 0, 2, jnp.where(i == 1, 1, jnp.where(i == 2, 3, 0)))
        block = lax.rem(z + dz, 4) * 2 + jnp.where(lax.rem(s, 2) == 0, 1 - x, x)
        where = pl.ds(pl.multiple_of(block * BLOCK, 128), BLOCK)
        part = lax.dot_general(
            normed[:, where], err[...], (((0,), (0,)), ((), ())), preferred_element_type=F32
        )
        grad[j, s] = part
        grad_half[j, s] = part.astype(BF16)

    def rs_copy(j, i, src, dst, device):
        return remote(src, dst, rs_send.at[j, i], rs_recv.at[j, i], device)

    def rs_sent(j, i, src):
        whole, count = src.dtype == F32, src.shape[0]

        def again():
            where = sibling_own.at[j] if whole else grad_half.at[j, 0, pl.ds(0, count)]
            return rs_copy(j, i, where, where, mate)

        sent.append(again)

    def rs_start(j, i, src, dst, device):
        rs_copy(j, i, src, dst, device).start()
        rs_sent(j, i, src)

    P_LAST, Q_LAST = pl.ds(0, half), pl.ds(half, q_rows // 2)

    def last_at(j, c, kind):
        rows = Q_LAST if kind % 2 else P_LAST
        return last_mate.at[j, c, rows] if kind > 3 else last.at[j, c, kind // 2, rows]

    def last_start(j, i, src, kind, h):
        device = (up_core, down_core, mate_core)[kind // 2][h]
        copy = remote(
            src, last_at(j, core, kind), rs_send.at[j, i], last_recv.at[j, core, kind], device
        )
        copy.start()
        rs_sent(j, i, src)

    def last_wait(j, c, kind):
        where = last_at(j, c, kind)
        remote(where, where, rs_send.at[j, 0], last_recv.at[j, c, kind], mate).wait_recv()

    def rs_wait(j, i, dst):
        rs_copy(j, i, dst, dst, mate).wait_recv()

    def out_of(j, s, part):
        return grad_half.at[j, s, pl.ds(*part)]

    far_p = ((0, half), (half, half))
    far_q = (2 * half, q_rows // 2)
    mate_pa, mate_pb = (0, half), (half, half)

    def near_at(j, d, part):
        return near.at[j, d, pl.ds(*part)]

    def far_at(j, d, part):
        return far.at[j, d, pl.ds(*part)]

    def scatter_q(j, i):
        if i < 3:
            rs_start(j, i, out_of(j, 2 * i, Q), from_mate.at[j, i], mate)
        else:
            last_start(j, 3, out_of(j, 6, QA), 5, 0)
            last_start(j, 25, out_of(j, 6, QB), 5, 1)

    def scatter_far(j):
        for c in range(2):
            rs_start(j, 4 + c, out_of(j, c, PA), far_at(j, 0, far_p[c]), up)
            rs_start(j, 6 + c, out_of(j, c, PB), far_at(j, 1, far_p[c]), down)

    def scatter_up(j):
        rs_start(j, 8, out_of(j, 2, PB), near_at(j, 0, mate_pb), up)
        last_start(j, 9, out_of(j, 3, PB), 0, 1)

    def scatter_down(j):
        rs_start(j, 10, out_of(j, 4, PA), near_at(j, 1, mate_pa), down)
        last_start(j, 11, out_of(j, 5, PA), 2, 0)

    def scatter_own(j):
        theirs = pl.ds(pl.multiple_of(other * ROWS, 64), ROWS)
        rs_start(j, 24, grad.at[j, 7, theirs], sibling_own.at[j], sibling)

    def added(j, s, part, terms):
        where = pl.ds(*part)
        value = grad[j, s, where, :]
        for term in terms:
            value = value + term[...].astype(F32)
        grad_half[j, s, where, :] = value.astype(BF16)
        return out_of(j, s, part)

    def relay_p(j):
        rs_wait(j, 4, far_at(j, 0, far_p[0]))
        rs_start(j, 12, added(j, 2, PA, [far_at(j, 0, far_p[0])]), near_at(j, 0, mate_pa), up)
        rs_wait(j, 6, far_at(j, 1, far_p[0]))
        rs_start(j, 14, added(j, 4, PB, [far_at(j, 1, far_p[0])]), near_at(j, 1, mate_pb), down)
        rs_wait(j, 5, far_at(j, 0, far_p[1]))
        last_start(j, 13, added(j, 3, PA, [far_at(j, 0, far_p[1])]), 0, 0)
        rs_wait(j, 7, far_at(j, 1, far_p[1]))
        last_start(j, 15, added(j, 5, PB, [far_at(j, 1, far_p[1])]), 2, 1)

    def mate_q(j, i, lower):
        start, count = (0, q_rows // 2) if lower else (q_rows // 2, q_rows // 2)
        return from_mate.at[j, i, pl.ds(start, count)]

    def far_q_send(j):
        rs_wait(j, 0, from_mate.at[j, 0])
        rs_start(j, 16, added(j, 1, QA, [mate_q(j, 0, True)]), far_at(j, 0, far_q), up)
        rs_start(j, 17, added(j, 1, QB, [mate_q(j, 0, False)]), far_at(j, 1, far_q), down)

    def near_q_up(j):
        rs_wait(j, 1, from_mate.at[j, 1])
        last_start(j, 18, added(j, 3, QB, [mate_q(j, 1, False)]), 1, 1)

    def near_q_down(j):
        rs_wait(j, 2, from_mate.at[j, 2])
        last_start(j, 19, added(j, 5, QA, [mate_q(j, 2, True)]), 3, 0)

    def relay_q(j):
        rs_wait(j, 16, far_at(j, 0, far_q))
        terms = [mate_q(j, 1, True), far_at(j, 0, far_q)]
        last_start(j, 20, added(j, 3, QA, terms), 1, 0)
        rs_wait(j, 17, far_at(j, 1, far_q))
        terms = [mate_q(j, 2, False), far_at(j, 1, far_q)]
        last_start(j, 21, added(j, 5, QB, terms), 3, 1)

    def mate_send(j):
        rs_wait(j, 12, near_at(j, 0, mate_pa))
        rs_wait(j, 10, near_at(j, 1, mate_pa))
        terms = [near_at(j, 0, mate_pa), near_at(j, 1, mate_pa)]
        last_start(j, 22, added(j, 6, PA, terms), 4, 0)
        rs_wait(j, 8, near_at(j, 0, mate_pb))
        rs_wait(j, 14, near_at(j, 1, mate_pb))
        terms = [near_at(j, 0, mate_pb), near_at(j, 1, mate_pb)]
        last_start(j, 23, added(j, 6, PB, terms), 4, 1)

    p_start, q_start = core * (q_rows // 2), other * half

    def most_of_total(j):
        rs_wait(j, 24, sibling_own.at[j])
        for k, c in enumerate((core, other)):
            for kind in (0, 2, 1, 3, 5):
                last_wait(j, c, kind)
            for start, rows, part in ((p_start, P_LAST, half), (q_start, Q_LAST, q_rows // 2)):
                here = pl.ds(pl.multiple_of(start, 16), part)
                if k:
                    value = sibling_own[j, here, :]
                else:
                    value = grad[j, 7, pl.ds(pl.multiple_of(core * ROWS + start, 16), part), :]
                value = value + last[j, c, 0, rows, :].astype(F32)
                value = value + last[j, c, 1, rows, :].astype(F32)
                if rows is Q_LAST:
                    value = value + last_mate[j, c, rows, :].astype(F32)
                total[j, k, here, :] = value

    def rest_of_total(j):
        for k, c in enumerate((core, other)):
            last_wait(j, c, 4)
            here = pl.ds(pl.multiple_of(p_start, 16), half)
            total[j, k, here, :] += last_mate[j, c, P_LAST, :].astype(F32)
            update(c, j, total[j, k])

    def update(c, j, gradient):
        columns = cols(c, j)
        fast = own_w[:, columns].astype(F32) - INNER_RATE * (gradient * scale)
        mixed = 0.5 * fast + 0.5 * partner[:, columns].astype(F32)
        base = anchor_v[:, columns]
        moment = SLOW_BETA * momentum_v[:, columns] + (base - mixed) / INNER_RATE
        new_momentum[:, columns] = moment
        new_anchor[:, columns] = base - OUTER_RATE * INNER_RATE * moment

    def drain():
        for copy in sent:
            copy().wait_send()
        sent.clear()

    def when(s, step, *todo):
        @pl.when(s == step)
        def _():
            for do in todo:
                do()

    def friend_part(i):
        if mask == 1:
            friend_swap(i).start()

    gather_own_x(0)
    gather_own_z(0)
    if mask != 1:
        for i in range(FRIEND_PARTS):
            friend_swap(i).start()
    friend_part(0)
    tgt_swap.start()
    gain_load.wait()

    @pl.loop(0, tiles)
    def _(i):
        norm_tile(i)

    gather_1(0)
    gather_1_rest(0)
    gather_2(0)
    gather_own_x(1)
    friend_part(1)
    gather_3(0)
    gather_own_z(1)
    gather_4(0)
    tgt_load.wait()

    @pl.loop(0, steps)
    def _(s):
        values_step(0, s)
        when(s, 0, lambda: gather_1(1))

    tgt_swap.wait_recv()

    @pl.loop(0, tiles)
    def _(i):
        tile_copy(other, i).wait_recv()

    @pl.loop(steps, 2 * steps)
    def _(s):
        values_step(0, s)
        when(s, steps, lambda: gather_1_rest(1))

    @pl.loop(0, 8)
    def _(s):
        grad_step(0, s)
        when(s, 1, lambda: gather_2(1), lambda: scatter_far(0), lambda: scatter_q(0, 0))
        when(
            s,
            3,
            lambda: gather_3(1),
            lambda: scatter_up(0),
            lambda: scatter_q(0, 1),
        )
        when(s, 5, lambda: scatter_q(0, 2), lambda: scatter_down(0))
        when(s, 7, lambda: scatter_own(0), lambda: scatter_q(0, 3), lambda: friend_part(2))

    gather_4(1)

    @pl.loop(0, 2 * steps)
    def _(s):
        values_step(1, s)
        when(s, 0, lambda: relay_p(0))
        when(s, 1, lambda: far_q_send(0))
        when(s, 3, lambda: near_q_up(0))

    @pl.loop(0, 8)
    def _(s):
        grad_step(1, s)
        when(s, 0, lambda: near_q_down(0))
        when(s, 1, lambda: scatter_far(1), lambda: scatter_q(1, 0))
        when(s, 2, lambda: mate_send(0))
        when(s, 3, lambda: scatter_up(1), lambda: scatter_q(1, 1), lambda: relay_q(0))
        when(s, 5, lambda: scatter_down(1), lambda: scatter_q(1, 2))
        when(s, 7, lambda: scatter_own(1), lambda: scatter_q(1, 3), lambda: friend_part(3))

    own_w_load.wait()
    anchor_load.wait()
    momentum_load.wait()
    if mask != 1:
        for i in range(FRIEND_PARTS):
            friend_swap(i).wait_recv()
    relay_p(1)
    far_q_send(1)
    near_q_up(1)
    mate_send(1)
    near_q_down(1)
    relay_q(1)
    if mask == 1:
        for i in range(FRIEND_PARTS):
            friend_swap(i).wait_recv()
    most_of_total(0)
    rest_of_total(0)
    most_of_total(1)

    for j in range(CHUNKS):
        w_swap(j).wait_send()
    tgt_swap.wait_send()
    for i in range(FRIEND_PARTS):
        friend_swap(i).wait_send()

    @pl.loop(0, tiles)
    def _(i):
        tile_copy(core, i).wait_send()

    drain()
    rest_of_total(1)


def run(mask, p_gather, p_rows, collective_id, tokens, target, gain, weights, previous, anchor, momentum):
    rows, width = tokens.shape
    kv = target.shape[1]
    half, q_rows = p_rows // 2, BLOCK - p_rows
    anywhere = pl.BlockSpec(memory_space=pltpu.HBM)
    vmem, dma = pltpu.VMEM, pltpu.SemaphoreType.DMA
    side = CHUNKS * CHUNK
    return pl.pallas_call(
        functools.partial(kernel, mask, p_gather, p_rows),
        out_shape=(jax.ShapeDtypeStruct((ROWS, kv), F32),) * 2,
        in_specs=[anywhere] * 7,
        out_specs=(pl.BlockSpec(memory_space=pltpu.VMEM),) * 2,
        scratch_shapes=[
            vmem((2 * rows, width), BF16),
            vmem((CHUNKS, width, CHUNK), BF16),
            vmem((CHUNKS, 8, BLOCK, CHUNK), F32),
            vmem((CHUNKS, 8, BLOCK, CHUNK), BF16),
            vmem((2, rows, side), BF16),
            vmem((2 * rows, CHUNK), BF16),
            vmem((CHUNKS, 3, q_rows, CHUNK), BF16),
            vmem((CHUNKS, 2, p_rows + q_rows // 2, CHUNK), BF16),
            vmem((CHUNKS, 2, p_rows, CHUNK), BF16),
            vmem((CHUNKS, 2, 2, ROWS, CHUNK), BF16),
            vmem((CHUNKS, 2, ROWS, CHUNK), BF16),
            vmem((CHUNKS, 2, ROWS, CHUNK), F32),
            vmem((CHUNKS, ROWS, CHUNK), F32),
            vmem((ROWS, kv), BF16),
            vmem((ROWS, kv), BF16),
            vmem((ROWS, kv), F32),
            vmem((ROWS, kv), F32),
            vmem((1, width), F32),
            dma((CHUNKS, N_AG)),
            dma((CHUNKS, N_AG)),
            dma((CHUNKS, N_RS)),
            dma((CHUNKS, N_RS)),
            dma((CHUNKS, 2, 6)),
            dma((rows // TILE,)),
            dma((rows // TILE,)),
            dma((3 + FRIEND_PARTS,)),
            dma((3 + FRIEND_PARTS,)),
            dma((8 + rows // TILE,)),
        ],
        compiler_params=pltpu.CompilerParams(
            collective_id=collective_id,
            has_side_effects=True,
            vmem_limit_bytes=56 << 20,
        ),
    )(tokens, target, gain, weights, previous, anchor, momentum)


def hand_over(moment, anchor, moment_out, anchor_out, sems):
    copies = [
        pltpu.make_async_copy(moment, moment_out, sems.at[0]),
        pltpu.make_async_copy(anchor, anchor_out, sems.at[1]),
    ]
    for copy in copies:
        copy.start()
    for copy in copies:
        copy.wait()


def results(moment, anchor):
    return pl.pallas_call(
        hand_over,
        out_shape=(jax.ShapeDtypeStruct(moment.shape, F32),) * 2,
        in_specs=[pl.BlockSpec(memory_space=pl.ANY)] * 2,
        out_specs=(pl.BlockSpec(memory_space=pltpu.HBM),) * 2,
        scratch_shapes=[pltpu.SemaphoreType.DMA((2,))],
    )(moment, anchor)


def shards(step_bit, tokens, target, norm_gain, weights, previous, anchor, momentum):
    bit_count = lax.axis_size("rep").bit_length() - 1
    chosen_bit = jnp.remainder(step_bit, jnp.int32(bit_count))
    branches = [
        functools.partial(run, 2**bit, *(SPLIT_X if bit == 0 else SPLIT), bit)
        for bit in range(bit_count)
    ]
    moment_new, anchor_new = lax.switch(
        chosen_bit,
        branches,
        tokens[0],
        target[0],
        norm_gain[None],
        weights[0],
        previous[0],
        anchor[0],
        momentum[0],
    )
    moment_new, anchor_new = results(moment_new, anchor_new)
    return (moment_new[None], anchor_new[None])


def solution(mesh):
    placed = (
        P(),
        P("rep", "fsdp", None),
        P("rep", "fsdp", None),
        P(),
        P("rep", "fsdp", None),
        P("rep", "fsdp", None),
        P("rep", "fsdp", None),
        P("rep", "fsdp", None),
    )
    return jax.shard_map(
        shards,
        mesh=mesh,
        in_specs=placed,
        out_specs=(P("rep", "fsdp", None), P("rep", "fsdp", None)),
        check_vma=False,
    )
```

```python
import functools

import jax
import jax.numpy as jnp
from jax import lax
from jax.experimental import pallas as pl
from jax.experimental.pallas import tpu as pltpu
from jax.sharding import PartitionSpec as P

EPS = 1e-06
INNER_RATE = 0.05
OUTER_RATE = 1.0
SLOW_BETA = 0.6

MESH = pl.DeviceIdType.MESH
BF16 = jnp.bfloat16
F32 = jnp.float32

ROWS = 320
BLOCK = 2 * ROWS
CHUNK = 256
CHUNKS = 2
FRIEND_PARTS = 4
SPLIT = (352, 352)
SPLIT_X = (416, 416)
TILE = 128
STEP = 512
N_AG = 20
N_RS = 26


def kernel(
    mask,
    p_gather,
    p_rows,
    tokens,
    target,
    gain,
    weights,
    previous,
    anchor,
    momentum,
    new_momentum,
    new_anchor,
    normed,
    full,
    grad,
    grad_half,
    tgt,
    err,
    from_mate,
    far,
    near,
    last,
    last_mate,
    total,
    sibling_own,
    own_w,
    partner,
    anchor_v,
    momentum_v,
    gain_v,
    ag_send,
    ag_recv,
    rs_send,
    rs_recv,
    last_recv,
    n_send,
    n_recv,
    m_send,
    m_recv,
    local,
):
    rep = lax.axis_index("rep")
    at = lax.axis_index("fsdp")
    core = lax.rem(at, 2)
    other = 1 - core
    x = lax.rem(at // 2, 2)
    z = at // 4
    z_up, z_down, z_far = lax.rem(z + 1, 4), lax.rem(z + 3, 4), lax.rem(z + 2, 4)
    up, up_other = [(rep, z_up * 4 + x * 2 + c) for c in (core, other)]
    down, down_other = [(rep, z_down * 4 + x * 2 + c) for c in (core, other)]
    mate, mate_other = [(rep, z * 4 + (1 - x) * 2 + c) for c in (core, other)]
    up_core = [(rep, z_up * 4 + x * 2 + c) for c in range(2)]
    down_core = [(rep, z_down * 4 + x * 2 + c) for c in range(2)]
    mate_core = [(rep, z * 4 + (1 - x) * 2 + c) for c in range(2)]
    sibling = (rep, z * 4 + x * 2 + other)
    friend = (rep + mask - 2 * mask * lax.rem(rep // mask, 2), at)

    tokens_here, width = tokens.shape
    scale = width ** (-0.5)
    half = p_rows // 2
    q_rows = BLOCK - p_rows
    PA, PB = (0, half), (BLOCK - half, half)
    QA, QB, Q = (half, q_rows // 2), (ROWS, q_rows // 2), (half, q_rows)

    def remote(src, dst, send, recv, device):
        return pltpu.make_async_remote_copy(
            src_ref=src,
            dst_ref=dst,
            send_sem=send,
            recv_sem=recv,
            device_id=device,
            device_id_type=MESH,
        )

    sent = []

    barrier = pltpu.get_barrier_semaphore()
    everyone = (up, up_other, down, down_other, mate, mate_other, sibling, friend)
    for device in everyone:
        pl.semaphore_signal(barrier, inc=1, device_id=device, device_id_type=MESH)

    def load(src, dst, i):
        copy = pltpu.make_async_copy(src, dst, local.at[i])
        copy.start()
        return copy

    def cols(c, j):
        return pl.ds(pl.multiple_of(c * CHUNKS * CHUNK + j * CHUNK, CHUNK), CHUNK)

    def half_cols(c):
        return pl.ds(pl.multiple_of(c * CHUNKS * CHUNK, CHUNK), CHUNKS * CHUNK)

    own_base = (z * 2 + x) * BLOCK

    def own_rows(c):
        return pl.ds(pl.multiple_of(own_base + c * ROWS, 64), ROWS)

    w_loads = [
        load(weights.at[:, cols(core, j)], full.at[j, own_rows(core)], j)
        for j in range(CHUNKS)
    ]
    tiles = tokens_here // TILE

    def tile_of(c, i):
        return pl.ds(pl.multiple_of(c * tokens_here + i * TILE, TILE), TILE)

    gain_load = load(gain, gain_v, 2)
    token_base = 8

    @pl.loop(0, tiles)
    def _(i):
        rows = pl.ds(pl.multiple_of(i * TILE, TILE), TILE)
        pltpu.make_async_copy(
            tokens.at[rows], normed.at[tile_of(core, i)], local.at[token_base + i]
        ).start()

    tgt_load = load(target.at[:, half_cols(core)], tgt.at[core], 3)
    own_w_load = load(weights, own_w, 4)
    anchor_load = load(anchor, anchor_v, 5)
    momentum_load = load(momentum, momentum_v, 6)

    pl.semaphore_wait(barrier, len(everyone))

    def w_swap(j):
        return remote(
            weights.at[:, cols(other, j)],
            full.at[j, own_rows(core)],
            m_send.at[j],
            m_recv.at[j],
            sibling,
        )
    tgt_swap = remote(
        target.at[:, half_cols(other)], tgt.at[core], m_send.at[2], m_recv.at[2], sibling
    )
    friend_rows = ROWS // FRIEND_PARTS

    def friend_swap(i):
        where = pl.ds(i * friend_rows, friend_rows)
        return remote(
            previous.at[where], partner.at[where], m_send.at[3 + i], m_recv.at[3 + i], friend
        )

    def piece(j, zz, xx, part):
        start = pl.multiple_of((zz * 2 + xx) * BLOCK + part[0], 16)
        return full.at[j, pl.ds(start, part[1])]

    def ag_copy(j, i, zz, xx, part, device):
        where = piece(j, zz, xx, part)
        return remote(where, where, ag_send.at[j, i], ag_recv.at[j, i], device)

    def ag_start(j, i, zz, xx, part, device):
        ag_copy(j, i, zz, xx, part, device).start()
        sent.append(lambda: ag_copy(j, i, z, x, (0, part[1]), mate))

    def ag_wait(j, i, zz, xx, part):
        ag_copy(j, i, zz, xx, part, mate).wait_recv()

    xm = 1 - x

    def own_copy(j, i, c, device):
        return remote(
            weights.at[:, cols(c, j)],
            full.at[j, own_rows(core)],
            ag_send.at[j, i + jnp.where(c == core, 0, 1)],
            ag_recv.at[j, i + core],
            device,
        )

    def own_start(j, i, *targets):
        for c, device in targets:
            own_copy(j, i, c, device).start()
            sent.append(lambda c=c, device=device: own_copy(j, i, c, device))

    def own_wait(j, i, zz, xx, h):
        where = piece(j, zz, xx, half_of(h))
        remote(where, where, ag_send.at[j, i], ag_recv.at[j, i + h], mate).wait_recv()

    p_half = p_gather // 2
    q_half = ROWS - p_half

    def p_of(h):
        return (h * (BLOCK - p_half), p_half)

    def q_of(h):
        return (p_half + h * q_half, q_half)

    def half_of(h):
        return (h * ROWS, ROWS)

    def gather_own_z(j):
        own_start(j, 2, (core, up), (other, up_other))
        own_start(j, 4, (other, down_other), (core, down))

    def gather_own_x(j):
        own_start(j, 0, (core, mate), (other, mate_other))
        w_swap(j).start()

    def gather_1(j):
        own_wait(j, 2, z_down, x, core)
        ag_start(j, 10, z_down, x, half_of(core), up)
        ag_start(j, 12, z_down, x, q_of(core), mate)
        own_wait(j, 4, z_up, x, other)
        ag_start(j, 11, z_up, x, half_of(other), down)
        ag_start(j, 15, z_up, x, q_of(other), mate)
        own_wait(j, 0, z, xm, core)
        ag_start(j, 6, z, xm, p_of(core), up)

    def gather_1_rest(j):
        own_wait(j, 0, z, xm, other)
        ag_start(j, 9, z, xm, p_of(other), down)
        ag_start(j, 8, z, xm, p_of(other), up)
        ag_start(j, 7, z, xm, p_of(core), down)
        own_wait(j, 2, z_down, x, other)
        ag_start(j, 13, z_down, x, q_of(other), mate)
        own_wait(j, 4, z_up, x, core)
        ag_start(j, 14, z_up, x, q_of(core), mate)

    def gather_2(j):
        ag_wait(j, 10, z_far, x, half_of(core))
        ag_start(j, 16, z_far, x, q_of(core), mate)
        ag_wait(j, 11, z_far, x, half_of(other))
        ag_start(j, 17, z_far, x, q_of(other), mate)

    def gather_3(j):
        ag_wait(j, 6, z_down, xm, p_of(core))
        ag_start(j, 18, z_down, xm, p_of(core), up)
        ag_wait(j, 9, z_up, xm, p_of(other))
        ag_start(j, 19, z_up, xm, p_of(other), down)

    def gather_4(j):
        w_loads[j].wait()
        w_swap(j).wait_recv()
        ag_wait(j, 7, z_up, xm, p_of(core))
        ag_wait(j, 8, z_down, xm, p_of(other))
        ag_wait(j, 12, z_down, xm, q_of(core))
        ag_wait(j, 13, z_down, xm, q_of(other))
        ag_wait(j, 14, z_up, xm, q_of(core))
        ag_wait(j, 15, z_up, xm, q_of(other))
        ag_wait(j, 16, z_far, xm, q_of(core))
        ag_wait(j, 17, z_far, xm, q_of(other))
        ag_wait(j, 18, z_far, xm, p_of(core))
        ag_wait(j, 19, z_far, xm, p_of(other))

    def tile_copy(c, i):
        where = normed.at[tile_of(c, i)]
        return remote(where, where, n_send.at[i], n_recv.at[i], sibling)

    def norm_tile(i):
        where = tile_of(core, i)
        pltpu.make_async_copy(
            normed.at[where], normed.at[where], local.at[token_base + i]
        ).wait()
        for part in range(2):
            rows = pl.ds(
                pl.multiple_of(core * tokens_here + i * TILE + part * (TILE // 2), 64),
                TILE // 2,
            )
            value = normed[rows, :].astype(F32)
            rms = lax.rsqrt(jnp.mean(value * value, axis=-1, keepdims=True) + EPS)
            normed[rows, :] = (value * rms * gain_v[...]).astype(BF16)
        tile_copy(core, i).start()

    steps = tokens_here // STEP

    def values_step(j, s):
        side = jnp.where(s < steps, core, other)
        inner = lax.rem(s, steps) * STEP
        rows = pl.ds(pl.multiple_of(side * tokens_here + inner, STEP), STEP)
        values = jnp.dot(normed[rows, :], full[j], preferred_element_type=F32) * scale
        goal = tgt[
            side, pl.ds(pl.multiple_of(inner, STEP), STEP), j * CHUNK : (j + 1) * CHUNK
        ].astype(F32)
        err[rows, :] = (values - goal).astype(BF16)

    def grad_step(j, s):
        i = s // 2
        dz = jnp.where(i == 0, 2, jnp.where(i == 1, 1, jnp.where(i == 2, 3, 0)))
        block = lax.rem(z + dz, 4) * 2 + jnp.where(lax.rem(s, 2) == 0, 1 - x, x)
        where = pl.ds(pl.multiple_of(block * BLOCK, 128), BLOCK)
        part = lax.dot_general(
            normed[:, where], err[...], (((0,), (0,)), ((), ())), preferred_element_type=F32
        )
        grad[j, s] = part
        grad_half[j, s] = part.astype(BF16)

    def rs_copy(j, i, src, dst, device):
        return remote(src, dst, rs_send.at[j, i], rs_recv.at[j, i], device)

    def rs_sent(j, i, src):
        whole, count = src.dtype == F32, src.shape[0]

        def again():
            where = sibling_own.at[j] if whole else grad_half.at[j, 0, pl.ds(0, count)]
            return rs_copy(j, i, where, where, mate)

        sent.append(again)

    def rs_start(j, i, src, dst, device):
        rs_copy(j, i, src, dst, device).start()
        rs_sent(j, i, src)

    P_LAST, Q_LAST = pl.ds(0, half), pl.ds(half, q_rows // 2)

    def last_at(j, c, kind):
        rows = Q_LAST if kind % 2 else P_LAST
        return last_mate.at[j, c, rows] if kind > 3 else last.at[j, c, kind // 2, rows]

    def last_start(j, i, src, kind, h):
        device = (up_core, down_core, mate_core)[kind // 2][h]
        copy = remote(
            src, last_at(j, core, kind), rs_send.at[j, i], last_recv.at[j, core, kind], device
        )
        copy.start()
        rs_sent(j, i, src)

    def last_wait(j, c, kind):
        where = last_at(j, c, kind)
        remote(where, where, rs_send.at[j, 0], last_recv.at[j, c, kind], mate).wait_recv()

    def rs_wait(j, i, dst):
        rs_copy(j, i, dst, dst, mate).wait_recv()

    def out_of(j, s, part):
        return grad_half.at[j, s, pl.ds(*part)]

    far_p = ((0, half), (half, half))
    far_q = (2 * half, q_rows // 2)
    mate_pa, mate_pb = (0, half), (half, half)

    def near_at(j, d, part):
        return near.at[j, d, pl.ds(*part)]

    def far_at(j, d, part):
        return far.at[j, d, pl.ds(*part)]

    def scatter_q(j, i):
        if i < 3:
            rs_start(j, i, out_of(j, 2 * i, Q), from_mate.at[j, i], mate)
        else:
            last_start(j, 3, out_of(j, 6, QA), 5, 0)
            last_start(j, 25, out_of(j, 6, QB), 5, 1)

    def scatter_far(j):
        for c in range(2):
            rs_start(j, 4 + c, out_of(j, c, PA), far_at(j, 0, far_p[c]), up)
            rs_start(j, 6 + c, out_of(j, c, PB), far_at(j, 1, far_p[c]), down)

    def scatter_up(j):
        rs_start(j, 8, out_of(j, 2, PB), near_at(j, 0, mate_pb), up)
        last_start(j, 9, out_of(j, 3, PB), 0, 1)

    def scatter_down(j):
        rs_start(j, 10, out_of(j, 4, PA), near_at(j, 1, mate_pa), down)
        last_start(j, 11, out_of(j, 5, PA), 2, 0)

    def scatter_own(j):
        theirs = pl.ds(pl.multiple_of(other * ROWS, 64), ROWS)
        rs_start(j, 24, grad.at[j, 7, theirs], sibling_own.at[j], sibling)

    def added(j, s, part, terms):
        where = pl.ds(*part)
        value = grad[j, s, where, :]
        for term in terms:
            value = value + term[...].astype(F32)
        grad_half[j, s, where, :] = value.astype(BF16)
        return out_of(j, s, part)

    def relay_p(j):
        rs_wait(j, 4, far_at(j, 0, far_p[0]))
        rs_start(j, 12, added(j, 2, PA, [far_at(j, 0, far_p[0])]), near_at(j, 0, mate_pa), up)
        rs_wait(j, 6, far_at(j, 1, far_p[0]))
        rs_start(j, 14, added(j, 4, PB, [far_at(j, 1, far_p[0])]), near_at(j, 1, mate_pb), down)
        rs_wait(j, 5, far_at(j, 0, far_p[1]))
        last_start(j, 13, added(j, 3, PA, [far_at(j, 0, far_p[1])]), 0, 0)
        rs_wait(j, 7, far_at(j, 1, far_p[1]))
        last_start(j, 15, added(j, 5, PB, [far_at(j, 1, far_p[1])]), 2, 1)

    def mate_q(j, i, lower):
        start, count = (0, q_rows // 2) if lower else (q_rows // 2, q_rows // 2)
        return from_mate.at[j, i, pl.ds(start, count)]

    def far_q_send(j):
        rs_wait(j, 0, from_mate.at[j, 0])
        rs_start(j, 16, added(j, 1, QA, [mate_q(j, 0, True)]), far_at(j, 0, far_q), up)
        rs_start(j, 17, added(j, 1, QB, [mate_q(j, 0, False)]), far_at(j, 1, far_q), down)

    def near_q_up(j):
        rs_wait(j, 1, from_mate.at[j, 1])
        last_start(j, 18, added(j, 3, QB, [mate_q(j, 1, False)]), 1, 1)

    def near_q_down(j):
        rs_wait(j, 2, from_mate.at[j, 2])
        last_start(j, 19, added(j, 5, QA, [mate_q(j, 2, True)]), 3, 0)

    def relay_q(j):
        rs_wait(j, 16, far_at(j, 0, far_q))
        terms = [mate_q(j, 1, True), far_at(j, 0, far_q)]
        last_start(j, 20, added(j, 3, QA, terms), 1, 0)
        rs_wait(j, 17, far_at(j, 1, far_q))
        terms = [mate_q(j, 2, False), far_at(j, 1, far_q)]
        last_start(j, 21, added(j, 5, QB, terms), 3, 1)

    def mate_send(j):
        rs_wait(j, 12, near_at(j, 0, mate_pa))
        rs_wait(j, 10, near_at(j, 1, mate_pa))
        terms = [near_at(j, 0, mate_pa), near_at(j, 1, mate_pa)]
        last_start(j, 22, added(j, 6, PA, terms), 4, 0)
        rs_wait(j, 8, near_at(j, 0, mate_pb))
        rs_wait(j, 14, near_at(j, 1, mate_pb))
        terms = [near_at(j, 0, mate_pb), near_at(j, 1, mate_pb)]
        last_start(j, 23, added(j, 6, PB, terms), 4, 1)

    p_start, q_start = core * (q_rows // 2), other * half

    def most_of_total(j):
        rs_wait(j, 24, sibling_own.at[j])
        for k, c in enumerate((core, other)):
            for kind in (0, 2, 1, 3, 5):
                last_wait(j, c, kind)
            for start, rows, part in ((p_start, P_LAST, half), (q_start, Q_LAST, q_rows // 2)):
                here = pl.ds(pl.multiple_of(start, 16), part)
                if k:
                    value = sibling_own[j, here, :]
                else:
                    value = grad[j, 7, pl.ds(pl.multiple_of(core * ROWS + start, 16), part), :]
                value = value + last[j, c, 0, rows, :].astype(F32)
                value = value + last[j, c, 1, rows, :].astype(F32)
                if rows is Q_LAST:
                    value = value + last_mate[j, c, rows, :].astype(F32)
                if rows is Q_LAST:
                    update(c, j, here, value)
                else:
                    total[j, k, here, :] = value

    def rest_of_total(j):
        for k, c in enumerate((core, other)):
            last_wait(j, c, 4)
            here = pl.ds(pl.multiple_of(p_start, 16), half)
            update(c, j, here, total[j, k, here, :] + last_mate[j, c, P_LAST, :].astype(F32))

    def update(c, j, rows, gradient):
        columns = cols(c, j)
        fast = own_w[rows, columns].astype(F32) - INNER_RATE * (gradient * scale)
        mixed = 0.5 * fast + 0.5 * partner[rows, columns].astype(F32)
        base = anchor_v[rows, columns]
        moment = SLOW_BETA * momentum_v[rows, columns] + (base - mixed) / INNER_RATE
        new_momentum[rows, columns] = moment
        new_anchor[rows, columns] = base - OUTER_RATE * INNER_RATE * moment

    def drain():
        for copy in sent:
            copy().wait_send()
        sent.clear()

    def when(s, step, *todo):
        @pl.when(s == step)
        def _():
            for do in todo:
                do()

    def friend_part(i):
        if mask == 1:
            friend_swap(i).start()

    gather_own_x(0)
    gather_own_z(0)
    if mask != 1:
        for i in range(FRIEND_PARTS):
            friend_swap(i).start()
    friend_part(0)
    tgt_swap.start()
    gain_load.wait()

    @pl.loop(0, tiles)
    def _(i):
        norm_tile(i)

    gather_1(0)
    gather_1_rest(0)
    gather_2(0)
    gather_own_x(1)
    friend_part(1)
    gather_3(0)
    gather_own_z(1)
    gather_4(0)
    tgt_load.wait()

    @pl.loop(0, steps)
    def _(s):
        values_step(0, s)
        when(s, 0, lambda: gather_1(1))

    tgt_swap.wait_recv()

    @pl.loop(0, tiles)
    def _(i):
        tile_copy(other, i).wait_recv()

    @pl.loop(steps, 2 * steps)
    def _(s):
        values_step(0, s)
        when(s, steps, lambda: gather_1_rest(1))

    @pl.loop(0, 8)
    def _(s):
        grad_step(0, s)
        when(s, 1, lambda: gather_2(1), lambda: scatter_far(0), lambda: scatter_q(0, 0))
        when(
            s,
            3,
            lambda: gather_3(1),
            lambda: scatter_up(0),
            lambda: scatter_q(0, 1),
        )
        when(s, 5, lambda: scatter_q(0, 2), lambda: scatter_down(0))
        when(s, 7, lambda: scatter_own(0), lambda: scatter_q(0, 3), lambda: friend_part(2))

    gather_4(1)

    @pl.loop(0, 2 * steps)
    def _(s):
        values_step(1, s)
        when(s, 0, lambda: relay_p(0))
        when(s, 1, lambda: far_q_send(0))
        when(s, 3, lambda: near_q_up(0))

    @pl.loop(0, 8)
    def _(s):
        grad_step(1, s)
        when(s, 0, lambda: near_q_down(0))
        when(s, 1, lambda: scatter_far(1), lambda: scatter_q(1, 0))
        when(s, 2, lambda: mate_send(0))
        when(s, 3, lambda: scatter_up(1), lambda: scatter_q(1, 1), lambda: relay_q(0))
        when(s, 5, lambda: scatter_down(1), lambda: scatter_q(1, 2))
        when(s, 7, lambda: scatter_own(1), lambda: scatter_q(1, 3), lambda: friend_part(3))

    own_w_load.wait()
    anchor_load.wait()
    momentum_load.wait()
    if mask != 1:
        for i in range(FRIEND_PARTS):
            friend_swap(i).wait_recv()
    relay_p(1)
    far_q_send(1)
    near_q_up(1)
    mate_send(1)
    near_q_down(1)
    relay_q(1)
    if mask == 1:
        for i in range(FRIEND_PARTS):
            friend_swap(i).wait_recv()
    most_of_total(0)
    rest_of_total(0)
    most_of_total(1)

    for j in range(CHUNKS):
        w_swap(j).wait_send()
    tgt_swap.wait_send()
    for i in range(FRIEND_PARTS):
        friend_swap(i).wait_send()

    @pl.loop(0, tiles)
    def _(i):
        tile_copy(core, i).wait_send()

    drain()
    rest_of_total(1)


def run(mask, p_gather, p_rows, collective_id, tokens, target, gain, weights, previous, anchor, momentum):
    rows, width = tokens.shape
    kv = target.shape[1]
    half, q_rows = p_rows // 2, BLOCK - p_rows
    anywhere = pl.BlockSpec(memory_space=pltpu.HBM)
    vmem, dma = pltpu.VMEM, pltpu.SemaphoreType.DMA
    side = CHUNKS * CHUNK
    return pl.pallas_call(
        functools.partial(kernel, mask, p_gather, p_rows),
        out_shape=(jax.ShapeDtypeStruct((ROWS, kv), F32),) * 2,
        in_specs=[anywhere] * 7,
        out_specs=(pl.BlockSpec(memory_space=pltpu.VMEM),) * 2,
        scratch_shapes=[
            vmem((2 * rows, width), BF16),
            vmem((CHUNKS, width, CHUNK), BF16),
            vmem((CHUNKS, 8, BLOCK, CHUNK), F32),
            vmem((CHUNKS, 8, BLOCK, CHUNK), BF16),
            vmem((2, rows, side), BF16),
            vmem((2 * rows, CHUNK), BF16),
            vmem((CHUNKS, 3, q_rows, CHUNK), BF16),
            vmem((CHUNKS, 2, p_rows + q_rows // 2, CHUNK), BF16),
            vmem((CHUNKS, 2, p_rows, CHUNK), BF16),
            vmem((CHUNKS, 2, 2, ROWS, CHUNK), BF16),
            vmem((CHUNKS, 2, ROWS, CHUNK), BF16),
            vmem((CHUNKS, 2, ROWS, CHUNK), F32),
            vmem((CHUNKS, ROWS, CHUNK), F32),
            vmem((ROWS, kv), BF16),
            vmem((ROWS, kv), BF16),
            vmem((ROWS, kv), F32),
            vmem((ROWS, kv), F32),
            vmem((1, width), F32),
            dma((CHUNKS, N_AG)),
            dma((CHUNKS, N_AG)),
            dma((CHUNKS, N_RS)),
            dma((CHUNKS, N_RS)),
            dma((CHUNKS, 2, 6)),
            dma((rows // TILE,)),
            dma((rows // TILE,)),
            dma((3 + FRIEND_PARTS,)),
            dma((3 + FRIEND_PARTS,)),
            dma((8 + rows // TILE,)),
        ],
        compiler_params=pltpu.CompilerParams(
            collective_id=collective_id,
            has_side_effects=True,
            vmem_limit_bytes=56 << 20,
        ),
    )(tokens, target, gain, weights, previous, anchor, momentum)


def hand_over(moment, anchor, moment_out, anchor_out, sems):
    copies = [
        pltpu.make_async_copy(moment, moment_out, sems.at[0]),
        pltpu.make_async_copy(anchor, anchor_out, sems.at[1]),
    ]
    for copy in copies:
        copy.start()
    for copy in copies:
        copy.wait()


def results(moment, anchor):
    return pl.pallas_call(
        hand_over,
        out_shape=(jax.ShapeDtypeStruct(moment.shape, F32),) * 2,
        in_specs=[pl.BlockSpec(memory_space=pl.ANY)] * 2,
        out_specs=(pl.BlockSpec(memory_space=pltpu.HBM),) * 2,
        scratch_shapes=[pltpu.SemaphoreType.DMA((2,))],
    )(moment, anchor)


def shards(step_bit, tokens, target, norm_gain, weights, previous, anchor, momentum):
    bit_count = lax.axis_size("rep").bit_length() - 1
    chosen_bit = jnp.remainder(step_bit, jnp.int32(bit_count))
    branches = [
        functools.partial(run, 2**bit, *(SPLIT_X if bit == 0 else SPLIT), bit)
        for bit in range(bit_count)
    ]
    moment_new, anchor_new = lax.switch(
        chosen_bit,
        branches,
        tokens[0],
        target[0],
        norm_gain[None],
        weights[0],
        previous[0],
        anchor[0],
        momentum[0],
    )
    moment_new, anchor_new = results(moment_new, anchor_new)
    return (moment_new[None], anchor_new[None])


def solution(mesh):
    placed = (
        P(),
        P("rep", "fsdp", None),
        P("rep", "fsdp", None),
        P(),
        P("rep", "fsdp", None),
        P("rep", "fsdp", None),
        P("rep", "fsdp", None),
        P("rep", "fsdp", None),
    )
    return jax.shard_map(
        shards,
        mesh=mesh,
        in_specs=placed,
        out_specs=(P("rep", "fsdp", None), P("rep", "fsdp", None)),
        check_vma=False,
    )
```
